32 devices in a mesh: groups: 2 (over y), wide: 16 (over z, x, core).
Axes of the slice: x: 2, y: 2, z: 4, core: 2. Of those that a mesh axis runs over, the one named last changes fastest.
Arguments:
- prefill_state: bfloat16 [128, 128, 4096], P('groups', None, 'wide'), parts along dimension 0, may hold values from -6 to 6
- residual_in: bfloat16 [128, 4, 2048], P(('groups', 'wide')), parts along dimension 0, may hold values from -3 to 3
- queries: bfloat16 [128, 4, 2048], P(('groups', 'wide')), parts along dimension 0, may hold values from -6 to 6
- keys_in: bfloat16 [128, 4, 2048], P(('groups', 'wide')), parts along dimension 0, may hold values from -6 to 6
- values_in: bfloat16 [128, 4, 4096], P(('groups', 'wide')), parts along dimension 0, may hold values from -6 to 6
- gate_in: bfloat16 [128, 4, 4096], P(('groups', 'wide')), parts along dimension 0, may hold values from -6 to 6
- beta_rate: bfloat16 [128, 4, 32], P(('groups', 'wide')), parts along dimension 0, may hold values from 0.099609375 to 0.8984375
- decay_rate: bfloat16 [128, 4, 32], P(('groups', 'wide')), parts along dimension 0, may hold values from 0.3984375 to 1
- norm_gain: float32 [128], replicated, may hold values from 0.5 to 1.5
- out_weight: bfloat16 [4096, 2048], P('wide'), may hold values from -0.09375 to 0.09375
- post_gain: float32 [2048], replicated, may hold values from 0.5 to 1.5
- router_weight: bfloat16 [2048, 128], replicated, may hold values from -0.375 to 0.375
- expert_ids: int32 [128, 4, 10], P(('groups', 'wide')), parts along dimension 0, may hold values from 0 to 127, all different within a row; in each aligned block of 16 rows (0 to 15, 16 to 31, ..., all dimensions but the last counted through in order) at most 2 rows name the same one
- expert_gate: bfloat16 [128, 2048, 512], P('wide'), may hold values from -0.125 to 0.125
- expert_up: bfloat16 [128, 2048, 512], P('wide'), may hold values from -0.125 to 0.125
- expert_down: bfloat16 [128, 512, 2048], P('wide'), may hold values from -0.25 to 0.25
Outputs:
- mixed: bfloat16 [128, 4, 2048], P(('groups', 'wide')), parts along dimension 0
The draws below stay inside these ranges and needn't reach their ends.
There are 2 independent parts, one for each index of `groups`. The reference program is written for one: setup_inputs(seed, part) draws one part's arguments, and reference() takes and returns one part's arrays. A program takes and returns all parts, laid end to end along the dimension named above; an argument that names none is the same for every part. Nothing has to cross between parts.
Inputs may be any that keep to these rules, and one draw needn't show every extreme that they name: `expert_ids`: each row names 10 different experts. In each aligned block of 16 rows (the requests of one device at all steps) no expert is named by more than 2 rows, and in every draw some expert is named by exactly 2 rows of a block.
All inputs are finite; a program needn't handle non-finite values.
Results may differ from the reference program's by a relative error of at most 0.0051.
Values may be sent and summed in bfloat16 or wider, within the bound.
A program may use at most 192 MiB of HBM per device.

```python
import math
import jax
import jax.numpy as jnp
import numpy as np
from jax import lax

D = 2048
HK = 16
DK = 128
HV = 32
DV = 128
EFF = 512
TOPK = 10
EXPERTS = 128
STEPS = 4
REQ_DEV = 4
REQUESTS = 64
CAP = 2
N_WIDE = 16


def steps_of(stream_key, extent, split, low, high):
    level = 1.0
    for dim, parts in split:
        steps = jax.random.uniform(jax.random.fold_in(jax.random.fold_in(stream_key, 6), dim), (parts,), jnp.float32, low / len(split), high / len(split))
        level = level * jnp.repeat(jnp.exp(steps), extent[dim] // parts).reshape((-1,) + (1,) * (len(extent) - 1 - dim))
    return level


def deal_out(key, own, number, rows, number_of, top, most, slope):
    ranking = jax.random.permutation(key, number_of)
    heavy_load, common = shares(number_of, rows * top, most, slope, True), shares(number_of, rows * top, most, slope, False)
    places = jnp.arange(number_of)

    def named(tallies, rotation):
        used = int((tallies > 0).sum())
        fixed = max(1, used // 4)
        passed = fixed + (places - fixed + rotation * (used - fixed)) % max(1, number_of - fixed)
        return jnp.zeros((number_of,), jnp.int32).at[ranking[jnp.where(places < fixed, places, passed)]].set(jnp.asarray(tallies, jnp.int32))

    tallies = jnp.where(number % 4 == 0, named(heavy_load, number // 4), named(common, number - number // 4 - 1))
    mixed = jax.random.permutation(jax.random.fold_in(own, 3), number_of)
    donor, taker = mixed[0:number_of // 2 * 2:2], mixed[1:number_of // 2 * 2:2]
    slack = jnp.minimum(tallies[donor] - 1, most - tallies[taker]) // 2
    slack = jnp.where((donor == ranking[0]) | (taker == ranking[0]) | (tallies[taker] == 0), 0, jnp.maximum(slack, 0))
    passed = jax.random.randint(jax.random.fold_in(own, 4), (number_of // 2,), 0, 1 << 20) % (slack + 1)
    tallies = tallies.at[donor].add(-passed).at[taker].add(passed)
    labels = jnp.searchsorted(jnp.cumsum(tallies), jnp.arange(rows * top), side="right").astype(jnp.int32)
    listing = labels.reshape(top, rows).T
    listing = listing[jax.random.permutation(jax.random.fold_in(own, 1), rows)]
    rotation = jax.random.randint(jax.random.fold_in(own, 2), (rows, 1), 0, top)
    return jnp.take_along_axis(listing, (jnp.arange(top)[None, :] + rotation) % top, axis=1)


def shares(amount, total, reach, skew, full):
    loads = [(1 << 20) // math.isqrt(grade ** skew) + 1 for grade in range(1, amount + 1)]
    largest = reach if full else min(reach, max(-(-total // amount), total * loads[0] // sum(loads)))
    least = 1 if total - largest >= amount - 1 else 0
    given, spare = [largest] + [least] * (amount - 1), total - largest - least * (amount - 1)
    while spare > 0:
        candidates = [i for i in range(1, amount) if given[i] < largest] or [i for i in range(1, amount) if given[i] < reach]
        whole, left = sum([loads[i] for i in candidates]), spare
        for i in candidates:
            extra = min(reach - given[i], max(1, left * loads[i] // whole), spare)
            given[i] = given[i] + extra
            spare = spare - extra
    return np.array(given)


def scatter_about(key, shape, width, bound, shards=(), kind=jnp.bfloat16):
    entries = width * jax.random.normal(key, shape, jnp.float32)
    if shards:
        entries = entries * steps_of(key, shape, shards, -0.22, 0.18)
    return jnp.clip(entries, -bound, bound).astype(kind)


def setup_inputs(seed: int = 0, part: int = 0) -> dict:
    keys = jax.random.split(jax.random.key(seed), 17)
    part_keys = jax.random.split(jax.random.fold_in(keys[16], part), 17)
    prefill_state = scatter_about(part_keys[0], (REQUESTS, DK, HV * DV), 1.0, 6.0, ((2, 16),))
    residual_in = scatter_about(part_keys[1], (REQUESTS, STEPS, D), 0.5, 3.0, ((0, 16),))
    queries = scatter_about(part_keys[2], (REQUESTS, STEPS, HK * DK), 1.0, 6.0, ((0, 16),))
    keys_in = scatter_about(part_keys[3], (REQUESTS, STEPS, HK * DK), 1.0, 6.0, ((0, 16),))
    values_in = scatter_about(part_keys[4], (REQUESTS, STEPS, HV * DV), 1.0, 6.0, ((0, 16),))
    gate_in = scatter_about(part_keys[5], (REQUESTS, STEPS, HV * DV), 1.0, 6.0, ((0, 16),))
    beta_rate = jnp.clip(0.099609375 + 0.7988281 * jax.random.uniform(part_keys[6], (REQUESTS, STEPS, HV), jnp.float32) ** steps_of(part_keys[6], (REQUESTS, STEPS, HV), ((0, 16),), -0.2, 0.2), 0.099609375, 0.8984375).astype(jnp.bfloat16)
    decay_rate = jnp.clip(0.3984375 + 0.6015625 * jax.random.uniform(part_keys[7], (REQUESTS, STEPS, HV), jnp.float32) ** steps_of(part_keys[7], (REQUESTS, STEPS, HV), ((0, 16),), -0.2, 0.2), 0.3984375, 1.0).astype(jnp.bfloat16)
    norm_gain = jnp.clip(1.0 + 0.1 * jax.random.normal(keys[8], (DV,), jnp.float32), 0.5, 1.5)
    out_weight = scatter_about(keys[9], (HV * DV, D), (HV * DV) ** -0.5, 0.09375, ((0, 16),))
    post_gain = jnp.clip(1.0 + 0.1 * jax.random.normal(keys[10], (D,), jnp.float32), 0.5, 1.5)
    router_weight = scatter_about(keys[11], (D, EXPERTS), (D // 9) ** -0.5, 0.375)
    expert_ids_keys = jax.random.split(jax.random.fold_in(part_keys[12], 1), REQUESTS * STEPS // (REQ_DEV * STEPS))
    expert_ids_turns = jax.random.permutation(jax.random.fold_in(part_keys[12], 3), REQUESTS * STEPS // (REQ_DEV * STEPS))
    expert_ids = jax.vmap(lambda own, number: deal_out(jax.random.fold_in(part_keys[12], 2), own, number, REQ_DEV * STEPS, EXPERTS, TOPK, CAP, 2))(expert_ids_keys, expert_ids_turns).reshape((REQUESTS, STEPS, TOPK))
    expert_gate = scatter_about(keys[13], (EXPERTS, D, EFF), D ** -0.5, 0.125, ((0, 16),))
    expert_up = scatter_about(keys[14], (EXPERTS, D, EFF), D ** -0.5, 0.125, ((0, 16),))
    expert_down = scatter_about(keys[15], (EXPERTS, EFF, D), EFF ** -0.5, 0.25, ((0, 16),))
    return {"prefill_state": prefill_state, "residual_in": residual_in, "queries": queries, "keys_in": keys_in, "values_in": values_in, "gate_in": gate_in, "beta_rate": beta_rate, "decay_rate": decay_rate, "norm_gain": norm_gain, "out_weight": out_weight, "post_gain": post_gain, "router_weight": router_weight, "expert_ids": expert_ids, "expert_gate": expert_gate, "expert_up": expert_up, "expert_down": expert_down}


def unit_rows(vectors):
    vectors = vectors.astype(jnp.float32)
    return vectors * lax.rsqrt(lax.optimization_barrier(jnp.sum(vectors * vectors, axis=-1, keepdims=True)) + 1e-06)

def recurrence(carry_state, q_unit, k_unit, value_cols, beta_cols, decay_cols):
    results = []
    for step_idx in range(q_unit.shape[1]):
        carry_state = carry_state * decay_cols[:, step_idx][:, None]
        key_now = jnp.swapaxes(k_unit[:, step_idx], 1, 2)[..., None]
        predicted = jnp.einsum('bdhc,bhd->bhc', carry_state, k_unit[:, step_idx], precision=lax.Precision.HIGHEST)
        change = beta_cols[:, step_idx] * (value_cols[:, step_idx] - predicted)
        carry_state = carry_state + key_now * change[:, None]
        results.append(jnp.einsum('bdhc,bhd->bhc', carry_state, q_unit[:, step_idx], precision=lax.Precision.HIGHEST))
    return jnp.stack(results, axis=1)

def reference(prefill_state, residual_in, queries, keys_in, values_in, gate_in, beta_rate, decay_rate, norm_gain, out_weight, post_gain, router_weight, expert_ids, expert_gate, expert_up, expert_down):
    block_rows = math.gcd(REQUESTS, 64)
    num_blocks = REQUESTS // block_rows
    key_group = 2 * DV

    def split_blocks(array):
        return array.reshape((num_blocks, block_rows) + array.shape[1:])

    def one_block(packed):
        state_in, query_b, key_b, value_b, gate_b, beta_b, decay_b = packed
        carry_state = state_in.astype(jnp.float32).reshape(block_rows, DK, HK, key_group)
        q_unit = unit_rows(query_b.reshape(block_rows, STEPS, HK, DK))
        k_unit = unit_rows(key_b.reshape(block_rows, STEPS, HK, DK))
        value_cols = value_b.astype(jnp.float32).reshape(block_rows, STEPS, HK, key_group)
        beta_cols = jnp.repeat(beta_b.astype(jnp.float32), DV, axis=-1).reshape(block_rows, STEPS, HK, key_group)
        decay_cols = jnp.repeat(decay_b.astype(jnp.float32), DV, axis=-1).reshape(block_rows, STEPS, HK, key_group)
        attended = recurrence(carry_state, q_unit, k_unit, value_cols, beta_cols, decay_cols)
        heads_view = attended.reshape(block_rows, STEPS, HV, DV)
        scale = lax.rsqrt(lax.optimization_barrier(jnp.mean(heads_view * heads_view, axis=-1, keepdims=True)) + 1e-06)
        gate_act = jax.nn.silu(gate_b.astype(jnp.float32).reshape(block_rows, STEPS, HV, DV))
        normed = (heads_view * scale * norm_gain * gate_act).astype(jnp.bfloat16)
        return normed.reshape(block_rows, STEPS, HV * DV)
    normed = lax.map(one_block, (split_blocks(prefill_state), split_blocks(queries), split_blocks(keys_in), split_blocks(values_in), split_blocks(gate_in), split_blocks(beta_rate), split_blocks(decay_rate)))
    total_rows = REQUESTS * STEPS
    normed = normed.reshape(total_rows, HV * DV)
    attention = jnp.dot(normed, out_weight, preferred_element_type=jnp.float32)
    hidden = residual_in.reshape(total_rows, D).astype(jnp.float32) + attention
    moe_in = (hidden * lax.rsqrt(lax.optimization_barrier(jnp.mean(hidden * hidden, axis=-1, keepdims=True)) + 1e-06) * post_gain).astype(jnp.bfloat16)
    logits = jnp.dot(moe_in, router_weight, preferred_element_type=jnp.float32)
    flat_ids = expert_ids.reshape(total_rows, TOPK).astype(jnp.int32)
    chosen = jnp.take_along_axis(logits, flat_ids, axis=1)
    squashed = jax.nn.sigmoid(chosen)
    gates = squashed / lax.optimization_barrier(jnp.sum(squashed, axis=1, keepdims=True))
    limit = min(CAP * N_WIDE, total_rows)

    def per_expert(total_out, packed):
        gate_w, up_w, down_w, index = packed
        hit_mask = flat_ids == index
        weight_row = lax.optimization_barrier(jnp.sum(jnp.where(hit_mask, gates, 0.0), axis=1))
        hit_rows = jnp.any(hit_mask, axis=1)
        row_order = jnp.argsort(jnp.where(hit_rows, 0, 1).astype(jnp.int32), stable=True)[:limit]
        chosen_in = moe_in[row_order]
        gate_act = jnp.dot(chosen_in, gate_w, preferred_element_type=jnp.float32)
        up_act = jnp.dot(chosen_in, up_w, preferred_element_type=jnp.float32)
        expert_mid = (jax.nn.silu(gate_act) * up_act).astype(jnp.bfloat16)
        expert_res = jnp.dot(expert_mid, down_w, preferred_element_type=jnp.float32).astype(jnp.bfloat16)
        total_out = total_out.at[row_order].add(weight_row[row_order][:, None] * expert_res.astype(jnp.float32))
        return (total_out, None)
    total_out, _ = lax.scan(per_expert, jnp.zeros((total_rows, D), jnp.float32), (expert_gate, expert_up, expert_down, jnp.arange(EXPERTS, dtype=jnp.int32)))
    return (hidden + total_out).astype(jnp.bfloat16).reshape(REQUESTS, STEPS, D)
```

```python
import jax
import jax.numpy as jnp
from jax import lax
from jax.sharding import PartitionSpec as P

TOPK = 10
CAP = 2


def unit_rows(vectors):
    vectors = vectors.astype(jnp.float32)
    return vectors * lax.rsqrt(jnp.sum(vectors * vectors, axis=-1, keepdims=True) + 1e-06)


def recurrence(carry_state, q_unit, k_unit, value_cols, beta_cols, decay_cols):
    results = []
    for step_idx in range(q_unit.shape[1]):
        carry_state = carry_state * decay_cols[:, step_idx][:, None]
        key_now = jnp.swapaxes(k_unit[:, step_idx], 1, 2)[..., None]
        predicted = jnp.einsum(
            "bdhc,bhd->bhc", carry_state, k_unit[:, step_idx], precision=lax.Precision.HIGHEST
        )
        change = beta_cols[:, step_idx] * (value_cols[:, step_idx] - predicted)
        carry_state = carry_state + key_now * change[:, None]
        results.append(
            jnp.einsum(
                "bdhc,bhd->bhc", carry_state, q_unit[:, step_idx], precision=lax.Precision.HIGHEST
            )
        )
    return jnp.stack(results, axis=1)


def local_heads(prefill_state, queries, keys_in, values_in, gate_in, beta_rate, decay_rate, norm_gain):
    owned_req, num_steps, _ = queries.shape
    total_req, key_dim, columns = prefill_state.shape
    head_dim = norm_gain.shape[0]
    wide_size = lax.axis_size("wide")
    group = columns // head_dim

    def by_head(array):
        return array.reshape(owned_req, num_steps, wide_size, -1)

    packed = jnp.concatenate(
        [by_head(a) for a in (queries, keys_in, values_in, gate_in, beta_rate, decay_rate)], axis=-1
    )
    got = lax.all_to_all(packed, "wide", split_axis=2, concat_axis=0, tiled=True)[:, :, 0]
    q_raw, k_raw, v_raw, g_raw, beta, decay = jnp.split(
        got,
        [key_dim, 2 * key_dim, 2 * key_dim + columns, 2 * key_dim + 2 * columns, 2 * key_dim + 2 * columns + group],
        axis=-1,
    )

    def inverse_norm(vectors):
        vectors = vectors.astype(jnp.float32)
        return lax.rsqrt(jnp.sum(vectors * vectors, axis=-1) + 1e-06)

    q_inv, k_inv = inverse_norm(q_raw), inverse_norm(k_raw)
    both = jnp.concatenate([k_raw, q_raw], axis=1)
    from_state = jnp.einsum("rsd,rdc->rsc", both, prefill_state, preferred_element_type=jnp.float32)
    gram = jnp.einsum("rsd,rtd->rst", both, k_raw, preferred_element_type=jnp.float32)
    gram = gram * jnp.concatenate([k_inv, q_inv], axis=1)[:, :, None] * k_inv[:, None, :]
    from_state = from_state * jnp.concatenate([k_inv, q_inv], axis=1)[:, :, None]

    def widen(rates):
        return jnp.repeat(rates.astype(jnp.float32), head_dim, axis=-1)

    beta, decay = widen(beta), widen(decay)
    value_cols = v_raw.astype(jnp.float32)
    through = jnp.ones_like(decay[:, 0])
    changes, results = [], []
    for t in range(num_steps):
        through = through * decay[:, t]
        changes = [c * decay[:, t] for c in changes]
        predicted = through * from_state[:, t]
        attended = through * from_state[:, num_steps + t]
        for s, c in enumerate(changes):
            predicted = predicted + gram[:, t, s][:, None] * c
            attended = attended + gram[:, num_steps + t, s][:, None] * c
        now = beta[:, t] * (value_cols[:, t] - predicted)
        attended = attended + gram[:, num_steps + t, t][:, None] * now
        changes.append(now)
        results.append(attended)
    heads_view = jnp.stack(results, axis=1).reshape(total_req * num_steps, group, head_dim)
    scale = lax.rsqrt(jnp.mean(heads_view * heads_view, axis=-1, keepdims=True) + 1e-06)
    gate_act = jax.nn.silu(g_raw.astype(jnp.float32)).reshape(heads_view.shape)
    normed = (heads_view * scale * norm_gain * gate_act).astype(jnp.bfloat16)
    return normed.reshape(total_req * num_steps, columns)


def moved_heads(prefill_state, queries, keys_in, values_in, gate_in, beta_rate, decay_rate, norm_gain):
    wide_size = lax.axis_size("wide")
    owned_req = queries.shape[0]
    num_steps = queries.shape[1]
    local_rows = owned_req * num_steps
    key_dim = prefill_state.shape[1]
    columns = prefill_state.shape[2]
    head_dim = norm_gain.shape[0]
    hv_dv = values_in.shape[2]
    value_heads = hv_dv // head_dim
    key_heads = queries.shape[2] // key_dim
    key_group = hv_dv // key_heads
    arrived = lax.all_to_all(prefill_state, "wide", split_axis=0, concat_axis=2, tiled=True)
    carry_state = arrived.astype(jnp.float32).reshape(owned_req, key_dim, key_heads, key_group)
    q_unit = unit_rows(queries.reshape(owned_req, num_steps, key_heads, key_dim))
    k_unit = unit_rows(keys_in.reshape(owned_req, num_steps, key_heads, key_dim))
    value_cols = values_in.astype(jnp.float32).reshape(owned_req, num_steps, key_heads, key_group)
    beta_cols = jnp.repeat(beta_rate.astype(jnp.float32), head_dim, axis=-1).reshape(
        owned_req, num_steps, key_heads, key_group
    )
    decay_cols = jnp.repeat(decay_rate.astype(jnp.float32), head_dim, axis=-1).reshape(
        owned_req, num_steps, key_heads, key_group
    )
    attended = recurrence(carry_state, q_unit, k_unit, value_cols, beta_cols, decay_cols).reshape(
        local_rows, hv_dv
    )
    heads_view = attended.reshape(local_rows, value_heads, head_dim)
    scale = lax.rsqrt(jnp.mean(heads_view * heads_view, axis=-1, keepdims=True) + 1e-06)
    gate_act = jax.nn.silu(gate_in.reshape(local_rows, value_heads, head_dim).astype(jnp.float32))
    normed = (
        (heads_view * scale * norm_gain * gate_act).astype(jnp.bfloat16).reshape(local_rows, hv_dv)
    )
    return lax.all_to_all(
        normed.reshape(local_rows, wide_size, columns),
        "wide",
        split_axis=1,
        concat_axis=0,
        tiled=True,
    ).reshape(wide_size * local_rows, columns)


def per_device(
    prefill_state,
    residual_in,
    queries,
    keys_in,
    values_in,
    gate_in,
    beta_rate,
    decay_rate,
    norm_gain,
    out_weight,
    post_gain,
    router_weight,
    expert_ids,
    expert_gate,
    expert_up,
    expert_down,
):
    wide_size = lax.axis_size("wide")
    owned_req = queries.shape[0]
    num_steps = queries.shape[1]
    local_rows = owned_req * num_steps
    key_dim = prefill_state.shape[1]
    columns = prefill_state.shape[2]
    head_dim = norm_gain.shape[0]
    hv_dv = values_in.shape[2]
    value_heads = hv_dv // head_dim
    key_heads = queries.shape[2] // key_dim
    key_group = hv_dv // key_heads
    width = residual_in.shape[2]
    heads = local_heads if key_heads == wide_size else moved_heads
    spread = heads(
        prefill_state, queries, keys_in, values_in, gate_in, beta_rate, decay_rate, norm_gain
    )
    attention = lax.psum_scatter(
        jnp.dot(spread, out_weight, preferred_element_type=jnp.float32),
        "wide",
        scatter_dimension=0,
        tiled=True,
    )
    hidden = residual_in.reshape(local_rows, width).astype(jnp.float32) + attention
    moe_in = (
        hidden * lax.rsqrt(jnp.mean(hidden * hidden, axis=-1, keepdims=True) + 1e-06) * post_gain
    ).astype(jnp.bfloat16)
    logits = jnp.dot(moe_in, router_weight, preferred_element_type=jnp.float32)
    num_experts = router_weight.shape[1]
    flat_ids = expert_ids.reshape(local_rows, TOPK)
    onehot = flat_ids[:, :, None] == jnp.arange(num_experts, dtype=jnp.int32)[None, None, :]
    chosen = jnp.sum(jnp.where(onehot, logits[:, None, :], 0.0), axis=-1)
    squashed = jax.nn.sigmoid(chosen)
    gates = squashed / jnp.sum(squashed, axis=1, keepdims=True)
    counts_flat = onehot.reshape(local_rows * TOPK, num_experts).astype(jnp.int32)
    running = jnp.cumsum(counts_flat, axis=0) - 1
    slot_of = jnp.sum(counts_flat * running, axis=1).reshape(local_rows, TOPK)
    position = flat_ids * CAP + slot_of
    dispatch = jnp.any(
        position[:, :, None] == jnp.arange(num_experts * CAP, dtype=jnp.int32)[None, None, :],
        axis=1,
    ).astype(jnp.bfloat16)
    buffer = jnp.einsum("rs,rd->sd", dispatch, moe_in, preferred_element_type=jnp.float32).astype(
        jnp.bfloat16
    )
    exp_dev = expert_gate.shape[0]
    buffer = buffer.reshape(wide_size, exp_dev, CAP, width)
    slab_in = lax.all_to_all(buffer, "wide", split_axis=0, concat_axis=0, tiled=True)
    gate_part = jnp.einsum(
        "sekd,edf->sekf", slab_in, expert_gate, preferred_element_type=jnp.float32
    )
    up_part = jnp.einsum("sekd,edf->sekf", slab_in, expert_up, preferred_element_type=jnp.float32)
    hidden_mid = (jax.nn.silu(gate_part) * up_part).astype(jnp.bfloat16)
    processed = jnp.einsum(
        "sekf,efd->sekd", hidden_mid, expert_down, preferred_element_type=jnp.float32
    ).astype(jnp.bfloat16)
    returned = lax.all_to_all(processed, "wide", split_axis=0, concat_axis=0, tiled=True).reshape(
        num_experts * CAP, width
    )
    picked = returned[position]
    combined = jnp.sum(gates[:, :, None] * picked.astype(jnp.float32), axis=1)
    return (hidden + combined).astype(jnp.bfloat16).reshape(owned_req, num_steps, width)


def solution(mesh):
    return jax.shard_map(
        per_device,
        mesh=mesh,
        in_specs=(
            P("groups", None, "wide"),
            P(("groups", "wide"), None, None),
            P(("groups", "wide"), None, None),
            P(("groups", "wide"), None, None),
            P(("groups", "wide"), None, None),
            P(("groups", "wide"), None, None),
            P(("groups", "wide"), None, None),
            P(("groups", "wide"), None, None),
            P(),
            P("wide", None),
            P(),
            P(),
            P(("groups", "wide"), None, None),
            P("wide", None, None),
            P("wide", None, None),
            P("wide", None, None),
        ),
        out_specs=P(("groups", "wide"), None, None),
        check_vma=False,
    )
```

```python
import functools

import jax
import jax.numpy as jnp
from jax import lax
from jax.experimental import pallas as pl
from jax.experimental.pallas import tpu as pltpu
from jax.sharding import PartitionSpec as P

TOPK = 10
CAP = 2


def unit_rows(vectors):
    vectors = vectors.astype(jnp.float32)
    return vectors * lax.rsqrt(jnp.sum(vectors * vectors, axis=-1, keepdims=True) + 1e-06)


def recurrence(carry_state, q_unit, k_unit, value_cols, beta_cols, decay_cols):
    results = []
    for step_idx in range(q_unit.shape[1]):
        carry_state = carry_state * decay_cols[:, step_idx][:, None]
        key_now = jnp.swapaxes(k_unit[:, step_idx], 1, 2)[..., None]
        predicted = jnp.einsum(
            "bdhc,bhd->bhc", carry_state, k_unit[:, step_idx], precision=lax.Precision.HIGHEST
        )
        change = beta_cols[:, step_idx] * (value_cols[:, step_idx] - predicted)
        carry_state = carry_state + key_now * change[:, None]
        results.append(
            jnp.einsum(
                "bdhc,bhd->bhc", carry_state, q_unit[:, step_idx], precision=lax.Precision.HIGHEST
            )
        )
    return jnp.stack(results, axis=1)


def local_heads(prefill_state, queries, keys_in, values_in, gate_in, beta_rate, decay_rate, norm_gain):
    owned_req, num_steps, _ = queries.shape
    total_req, key_dim, columns = prefill_state.shape
    head_dim = norm_gain.shape[0]
    wide_size = lax.axis_size("wide")
    group = columns // head_dim

    def by_head(array):
        return array.reshape(owned_req, num_steps, wide_size, -1)

    packed = jnp.concatenate(
        [by_head(a) for a in (queries, keys_in, values_in, gate_in, beta_rate, decay_rate)], axis=-1
    )
    got = lax.all_to_all(packed, "wide", split_axis=2, concat_axis=0, tiled=True)[:, :, 0]
    q_raw, k_raw, v_raw, g_raw, beta, decay = jnp.split(
        got,
        [key_dim, 2 * key_dim, 2 * key_dim + columns, 2 * key_dim + 2 * columns, 2 * key_dim + 2 * columns + group],
        axis=-1,
    )

    def inverse_norm(vectors):
        vectors = vectors.astype(jnp.float32)
        return lax.rsqrt(jnp.sum(vectors * vectors, axis=-1) + 1e-06)

    q_inv, k_inv = inverse_norm(q_raw), inverse_norm(k_raw)
    both = jnp.concatenate([k_raw, q_raw], axis=1)
    from_state = jnp.einsum("rsd,rdc->rsc", both, prefill_state, preferred_element_type=jnp.float32)
    gram = jnp.einsum("rsd,rtd->rst", both, k_raw, preferred_element_type=jnp.float32)
    gram = gram * jnp.concatenate([k_inv, q_inv], axis=1)[:, :, None] * k_inv[:, None, :]
    from_state = from_state * jnp.concatenate([k_inv, q_inv], axis=1)[:, :, None]

    def widen(rates):
        return jnp.repeat(rates.astype(jnp.float32), head_dim, axis=-1)

    beta, decay = widen(beta), widen(decay)
    value_cols = v_raw.astype(jnp.float32)
    through = jnp.ones_like(decay[:, 0])
    changes, results = [], []
    for t in range(num_steps):
        through = through * decay[:, t]
        changes = [c * decay[:, t] for c in changes]
        predicted = through * from_state[:, t]
        attended = through * from_state[:, num_steps + t]
        for s, c in enumerate(changes):
            predicted = predicted + gram[:, t, s][:, None] * c
            attended = attended + gram[:, num_steps + t, s][:, None] * c
        now = beta[:, t] * (value_cols[:, t] - predicted)
        attended = attended + gram[:, num_steps + t, t][:, None] * now
        changes.append(now)
        results.append(attended)
    heads_view = jnp.stack(results, axis=1).reshape(total_req * num_steps, group, head_dim)
    scale = lax.rsqrt(jnp.mean(heads_view * heads_view, axis=-1, keepdims=True) + 1e-06)
    gate_act = jax.nn.silu(g_raw.astype(jnp.float32)).reshape(heads_view.shape)
    normed = (heads_view * scale * norm_gain * gate_act).astype(jnp.bfloat16)
    return normed.reshape(total_req * num_steps, columns)


def moved_heads(prefill_state, queries, keys_in, values_in, gate_in, beta_rate, decay_rate, norm_gain):
    wide_size = lax.axis_size("wide")
    owned_req = queries.shape[0]
    num_steps = queries.shape[1]
    local_rows = owned_req * num_steps
    key_dim = prefill_state.shape[1]
    columns = prefill_state.shape[2]
    head_dim = norm_gain.shape[0]
    hv_dv = values_in.shape[2]
    value_heads = hv_dv // head_dim
    key_heads = queries.shape[2] // key_dim
    key_group = hv_dv // key_heads
    arrived = lax.all_to_all(prefill_state, "wide", split_axis=0, concat_axis=2, tiled=True)
    carry_state = arrived.astype(jnp.float32).reshape(owned_req, key_dim, key_heads, key_group)
    q_unit = unit_rows(queries.reshape(owned_req, num_steps, key_heads, key_dim))
    k_unit = unit_rows(keys_in.reshape(owned_req, num_steps, key_heads, key_dim))
    value_cols = values_in.astype(jnp.float32).reshape(owned_req, num_steps, key_heads, key_group)
    beta_cols = jnp.repeat(beta_rate.astype(jnp.float32), head_dim, axis=-1).reshape(
        owned_req, num_steps, key_heads, key_group
    )
    decay_cols = jnp.repeat(decay_rate.astype(jnp.float32), head_dim, axis=-1).reshape(
        owned_req, num_steps, key_heads, key_group
    )
    attended = recurrence(carry_state, q_unit, k_unit, value_cols, beta_cols, decay_cols).reshape(
        local_rows, hv_dv
    )
    heads_view = attended.reshape(local_rows, value_heads, head_dim)
    scale = lax.rsqrt(jnp.mean(heads_view * heads_view, axis=-1, keepdims=True) + 1e-06)
    gate_act = jax.nn.silu(gate_in.reshape(local_rows, value_heads, head_dim).astype(jnp.float32))
    normed = (
        (heads_view * scale * norm_gain * gate_act).astype(jnp.bfloat16).reshape(local_rows, hv_dv)
    )
    return lax.all_to_all(
        normed.reshape(local_rows, wide_size, columns),
        "wide",
        split_axis=1,
        concat_axis=0,
        tiled=True,
    ).reshape(wide_size * local_rows, columns)


def dot(left, right):
    return jnp.dot(left, right, preferred_element_type=jnp.float32)


def dot_nt(left, right):
    return lax.dot_general(
        left, right, (((1,), (1,)), ((), ())), preferred_element_type=jnp.float32
    )


def layer_kernel(
    sizes,
    heads_ref,
    out_w_ref,
    resid_ref,
    post_ref,
    router_ref,
    ids_ref,
    gate_hbm,
    up_hbm,
    down_hbm,
    mixed_ref,
    gate_w,
    up_w,
    down_w,
    core_send,
    core_recv,
    x_send,
    x_recv,
    z_send,
    z_recv,
    part,
    lane_part,
    hidden,
    tokens,
    slab,
    outcome,
    pick_hi,
    pick_lo,
    w_sem,
    rs_send_sem,
    rs_recv_sem,
    ag_send_sem,
    ag_recv_sem,
):
    wide_size, owned, width, experts, local_experts, held = sizes
    num_z = wide_size // 4
    rows = wide_size * owned
    half = rows // 2
    me = lax.axis_index("wide")
    core = lax.rem(me, 2)
    x = lax.rem(me // 2, 2)
    z = me // 4

    def device_at(at_z, at_x, at_core):
        return at_z * 4 + at_x * 2 + at_core

    def z_ahead(d):
        return lax.rem(z + d, num_z)

    def z_behind(d):
        return lax.rem(z + num_z - d, num_z)

    core_mate = device_at(z, x, 1 - core)
    x_mate = device_at(z, 1 - x, core)
    z_mates = [device_at(z_ahead(d), x, core) for d in range(1, num_z)]

    def weight_copies(e, slot):
        return [
            pltpu.make_async_copy(hbm.at[e], vmem.at[slot], w_sem.at[i, slot])
            for i, (hbm, vmem) in enumerate(((gate_hbm, gate_w), (up_hbm, up_w), (down_hbm, down_w)))
        ]

    for e in range(held):
        for copy in weight_copies(e, e):
            copy.start()

    barrier = pltpu.get_barrier_semaphore()
    for mate in [core_mate, x_mate] + z_mates:
        pl.semaphore_signal(
            barrier, inc=1, device_id={"wide": mate}, device_id_type=pl.DeviceIdType.MESH
        )
    pl.semaphore_wait(barrier, 1 + num_z)

    def remote(src, dst, send_sem, recv_sem, mate):
        return pltpu.make_async_remote_copy(
            src_ref=src,
            dst_ref=dst,
            send_sem=send_sem,
            recv_sem=recv_sem,
            device_id={"wide": mate},
            device_id_type=pl.DeviceIdType.MESH,
        )

    def reduce_scatter(turn, produce):
        def exchange(i, src, dst, mate):
            copy = remote(src, dst, rs_send_sem.at[turn, i], rs_recv_sem.at[turn, i], mate)
            copy.start()
            return copy

        core_send[turn] = produce(1 - core).astype(jnp.bfloat16).reshape(num_z, 2, owned, width)
        to_core = exchange(0, core_send.at[turn], core_recv.at[turn], core_mate)
        part[...] = produce(core).reshape(num_z, 2, owned, width)
        to_core.wait()
        x_send[turn] = (part[:, 1 - x] + core_recv[turn, :, 1 - x].astype(jnp.float32)).astype(
            jnp.bfloat16
        )
        to_x = exchange(1, x_send.at[turn], x_recv.at[turn], x_mate)
        lane_part[...] = part[:, x] + core_recv[turn, :, x].astype(jnp.float32)
        to_x.wait()
        to_z = []
        for d in range(1, num_z):
            at_z = z_ahead(d)
            z_send[turn, d - 1] = (
                lane_part[at_z] + x_recv[turn, at_z].astype(jnp.float32)
            ).astype(jnp.bfloat16)
            to_z.append(
                exchange(1 + d, z_send.at[turn, d - 1], z_recv.at[turn, d - 1], z_mates[d - 1])
            )
        total = lane_part[z] + x_recv[turn, z].astype(jnp.float32)
        for d in range(1, num_z):
            to_z[d - 1].wait()
            total = total + z_recv[turn, d - 1].astype(jnp.float32)
        return total

    def project(at_core):
        return dot(heads_ref[:, at_core].reshape(half, heads_ref.shape[-1]), out_w_ref[...])

    now = resid_ref[...].astype(jnp.float32) + reduce_scatter(0, project)
    hidden[...] = now
    moe_in = now * lax.rsqrt(jnp.mean(now * now, axis=-1, keepdims=True) + 1e-06) * post_ref[...]
    tokens[me, :, :width] = moe_in.astype(jnp.bfloat16)
    tokens[me, :, width:] = ids_ref[...]

    sent = []

    def pass_on(block, mate):
        copy = remote(
            tokens.at[block],
            tokens.at[block],
            ag_send_sem.at[len(sent)],
            ag_recv_sem.at[block],
            mate,
        )
        copy.start()
        sent.append(copy)

    def arrived(block, mate):
        remote(
            tokens.at[block], tokens.at[block], ag_send_sem.at[0], ag_recv_sem.at[block], mate
        ).wait_recv()

    for mate in z_mates:
        pass_on(me, mate)
    pass_on(me, x_mate)
    pass_on(me, core_mate)
    arrived(x_mate, x_mate)
    pass_on(x_mate, core_mate)
    for d in range(1, num_z):
        block = device_at(z_behind(d), x, core)
        arrived(block, x_mate)
        pass_on(block, x_mate)
        pass_on(block, core_mate)
    for d in range(1, num_z):
        block = device_at(z_behind(d), 1 - x, core)
        arrived(block, x_mate)
        pass_on(block, core_mate)
    for at_z in range(num_z):
        for at_x in range(2):
            arrived(device_at(at_z, at_x, 1 - core), core_mate)
    for copy in sent:
        copy.wait_send()

    everyone = tokens[...].reshape(rows, width + 128)
    all_in = everyone[:, :width]
    named = everyone[:, width:].astype(jnp.float32)
    logits = dot(all_in, router_ref[...])
    lanes = lax.broadcasted_iota(jnp.int32, (rows, experts), 1).astype(jnp.float32)
    squashed = jnp.zeros((rows, experts), jnp.float32)
    chosen = jnp.zeros((rows, experts), jnp.float32)
    for k in range(TOPK):
        chosen = jnp.where(named[:, k : k + 1] == lanes, 1.0, chosen)
    squashed = jnp.where(chosen > 0.5, jax.nn.sigmoid(logits), 0.0)
    gates = squashed / jnp.sum(squashed, axis=1, keepdims=True)
    gates_hi = gates.astype(jnp.bfloat16)
    gates_lo = (gates - gates_hi.astype(jnp.float32)).astype(jnp.bfloat16)
    mine = (
        lax.broadcasted_iota(jnp.int32, (local_experts, experts), 1)
        == lax.broadcasted_iota(jnp.int32, (local_experts, experts), 0) + me * local_experts
    )
    mine = jnp.where(mine, 1.0, 0.0).astype(jnp.bfloat16)
    hits = dot_nt(mine, chosen.astype(jnp.bfloat16))
    local_hi = dot_nt(mine, gates_hi)
    local_lo = dot_nt(mine, gates_lo)
    row_a = lax.broadcasted_iota(jnp.int32, (rows, rows), 0)
    row_b = lax.broadcasted_iota(jnp.int32, (rows, rows), 1)
    earlier = (row_a // owned == row_b // owned) & (row_a < row_b)
    rank = dot(hits.astype(jnp.bfloat16), jnp.where(earlier, 1.0, 0.0).astype(jnp.bfloat16))
    origin = lax.broadcasted_iota(jnp.int32, (local_experts, rows), 1) // owned
    place = jnp.where(hits > 0.5, (origin * CAP).astype(jnp.float32) + rank, -1.0)
    slots = CAP * wide_size
    slot_no = lax.broadcasted_iota(jnp.int32, (slots, rows), 0).astype(jnp.float32)
    takes, takes_hi, takes_lo = [], [], []
    for e in range(local_experts):
        taken = place[e : e + 1] == slot_no
        takes.append(jnp.where(taken, 1.0, 0.0))
        takes_hi.append(jnp.where(taken, local_hi[e : e + 1], 0.0))
        takes_lo.append(jnp.where(taken, local_lo[e : e + 1], 0.0))
    take = jnp.concatenate(takes, axis=0).astype(jnp.bfloat16)
    slab[...] = dot(take, all_in).astype(jnp.bfloat16).reshape(local_experts, slots, width)

    def back(pieces):
        turned = jnp.concatenate(pieces, axis=0).T.astype(jnp.bfloat16)
        return turned.reshape(num_z * 2, 2, owned, local_experts * slots)

    pick_hi[...] = back(takes_hi)
    pick_lo[...] = back(takes_lo)

    @pl.loop(0, local_experts)
    def _(e):
        slot = lax.rem(e, held)
        for copy in weight_copies(e, slot):
            copy.wait()
        came = slab[e]
        gate_part = dot(came, gate_w[slot])
        up_part = dot(came, up_w[slot])
        mid = (jax.nn.silu(gate_part) * up_part).astype(jnp.bfloat16)
        outcome[e] = dot(mid, down_w[slot]).astype(jnp.bfloat16)

        @pl.when(e + held < local_experts)
        def _():
            for copy in weight_copies(e + held, slot):
                copy.start()

    def combine(at_core):
        results = outcome[...].reshape(local_experts * slots, width)
        hi = pick_hi[:, at_core].reshape(half, local_experts * slots)
        lo = pick_lo[:, at_core].reshape(half, local_experts * slots)
        return dot(hi, results) + dot(lo, results)

    mixed_ref[...] = (reduce_scatter(1, combine) + hidden[...]).astype(mixed_ref.dtype)


def fused_layer(
    spread, residual_in, out_weight, post_gain, router_weight, expert_ids, expert_gate, expert_up, expert_down
):
    wide_size = lax.axis_size("wide")
    owned_req, num_steps, width = residual_in.shape
    owned = owned_req * num_steps
    rows = wide_size * owned
    columns = spread.shape[1]
    num_z = wide_size // 4
    experts = router_weight.shape[1]
    local_experts, _, hidden_units = expert_gate.shape
    held = min(local_experts, 6)
    slots = CAP * wide_size
    ids = jnp.pad(
        expert_ids.reshape(owned, TOPK), ((0, 0), (0, 128 - TOPK)), constant_values=-1
    ).astype(jnp.bfloat16)
    half16 = (2, num_z, 2, owned, width)
    bf16, f32 = jnp.bfloat16, jnp.float32
    vmem = pl.BlockSpec(memory_space=pltpu.VMEM)
    hbm = pl.BlockSpec(memory_space=pl.ANY)
    out = pl.pallas_call(
        functools.partial(
            layer_kernel, (wide_size, owned, width, experts, local_experts, held)
        ),
        out_shape=jax.ShapeDtypeStruct((owned, width), bf16),
        in_specs=[vmem] * 6 + [hbm] * 3,
        out_specs=vmem,
        scratch_shapes=[
            pltpu.VMEM((held, width, hidden_units), bf16),
            pltpu.VMEM((held, width, hidden_units), bf16),
            pltpu.VMEM((held, hidden_units, width), bf16),
            pltpu.VMEM(half16, bf16),
            pltpu.VMEM(half16, bf16),
            pltpu.VMEM((2, num_z, owned, width), bf16),
            pltpu.VMEM((2, num_z, owned, width), bf16),
            pltpu.VMEM((2, num_z - 1, owned, width), bf16),
            pltpu.VMEM((2, num_z - 1, owned, width), bf16),
            pltpu.VMEM((num_z, 2, owned, width), f32),
            pltpu.VMEM((num_z, owned, width), f32),
            pltpu.VMEM((owned, width), f32),
            pltpu.VMEM((wide_size, owned, width + 128), bf16),
            pltpu.VMEM((local_experts, slots, width), bf16),
            pltpu.VMEM((local_experts, slots, width), bf16),
            pltpu.VMEM((num_z * 2, 2, owned, local_experts * slots), bf16),
            pltpu.VMEM((num_z * 2, 2, owned, local_experts * slots), bf16),
            pltpu.SemaphoreType.DMA((3, held)),
            pltpu.SemaphoreType.DMA((2, 1 + num_z)),
            pltpu.SemaphoreType.DMA((2, 1 + num_z)),
            pltpu.SemaphoreType.DMA((wide_size,)),
            pltpu.SemaphoreType.DMA((wide_size,)),
        ],
        compiler_params=pltpu.CompilerParams(
            collective_id=0, has_side_effects=True, vmem_limit_bytes=60 * 1024 * 1024
        ),
    )(
        spread.reshape(num_z * 2, 2, owned, columns),
        out_weight,
        residual_in.reshape(owned, width),
        post_gain.reshape(1, width),
        router_weight,
        ids,
        expert_gate,
        expert_up,
        expert_down,
    )
    return out.reshape(owned_req, num_steps, width)


def per_device(
    prefill_state,
    residual_in,
    queries,
    keys_in,
    values_in,
    gate_in,
    beta_rate,
    decay_rate,
    norm_gain,
    out_weight,
    post_gain,
    router_weight,
    expert_ids,
    expert_gate,
    expert_up,
    expert_down,
):
    wide_size = lax.axis_size("wide")
    owned_req = queries.shape[0]
    num_steps = queries.shape[1]
    local_rows = owned_req * num_steps
    key_dim = prefill_state.shape[1]
    columns = prefill_state.shape[2]
    head_dim = norm_gain.shape[0]
    hv_dv = values_in.shape[2]
    value_heads = hv_dv // head_dim
    key_heads = queries.shape[2] // key_dim
    key_group = hv_dv // key_heads
    width = residual_in.shape[2]
    heads = local_heads if key_heads == wide_size else moved_heads
    spread = heads(
        prefill_state, queries, keys_in, values_in, gate_in, beta_rate, decay_rate, norm_gain
    )
    if key_heads == wide_size == 16 and local_rows == 16 and router_weight.shape[1] == 128:
        return fused_layer(
            spread,
            residual_in,
            out_weight,
            post_gain,
            router_weight,
            expert_ids,
            expert_gate,
            expert_up,
            expert_down,
        )
    attention = lax.psum_scatter(
        jnp.dot(spread, out_weight, preferred_element_type=jnp.float32),
        "wide",
        scatter_dimension=0,
        tiled=True,
    )
    hidden = residual_in.reshape(local_rows, width).astype(jnp.float32) + attention
    moe_in = (
        hidden * lax.rsqrt(jnp.mean(hidden * hidden, axis=-1, keepdims=True) + 1e-06) * post_gain
    ).astype(jnp.bfloat16)
    logits = jnp.dot(moe_in, router_weight, preferred_element_type=jnp.float32)
    num_experts = router_weight.shape[1]
    flat_ids = expert_ids.reshape(local_rows, TOPK)
    onehot = flat_ids[:, :, None] == jnp.arange(num_experts, dtype=jnp.int32)[None, None, :]
    chosen = jnp.sum(jnp.where(onehot, logits[:, None, :], 0.0), axis=-1)
    squashed = jax.nn.sigmoid(chosen)
    gates = squashed / jnp.sum(squashed, axis=1, keepdims=True)
    counts_flat = onehot.reshape(local_rows * TOPK, num_experts).astype(jnp.int32)
    running = jnp.cumsum(counts_flat, axis=0) - 1
    slot_of = jnp.sum(counts_flat * running, axis=1).reshape(local_rows, TOPK)
    position = flat_ids * CAP + slot_of
    dispatch = jnp.any(
        position[:, :, None] == jnp.arange(num_experts * CAP, dtype=jnp.int32)[None, None, :],
        axis=1,
    ).astype(jnp.bfloat16)
    buffer = jnp.einsum("rs,rd->sd", dispatch, moe_in, preferred_element_type=jnp.float32).astype(
        jnp.bfloat16
    )
    exp_dev = expert_gate.shape[0]
    buffer = buffer.reshape(wide_size, exp_dev, CAP, width)
    slab_in = lax.all_to_all(buffer, "wide", split_axis=0, concat_axis=0, tiled=True)
    gate_part = jnp.einsum(
        "sekd,edf->sekf", slab_in, expert_gate, preferred_element_type=jnp.float32
    )
    up_part = jnp.einsum("sekd,edf->sekf", slab_in, expert_up, preferred_element_type=jnp.float32)
    hidden_mid = (jax.nn.silu(gate_part) * up_part).astype(jnp.bfloat16)
    processed = jnp.einsum(
        "sekf,efd->sekd", hidden_mid, expert_down, preferred_element_type=jnp.float32
    ).astype(jnp.bfloat16)
    returned = lax.all_to_all(processed, "wide", split_axis=0, concat_axis=0, tiled=True).reshape(
        num_experts * CAP, width
    )
    picked = returned[position]
    combined = jnp.sum(gates[:, :, None] * picked.astype(jnp.float32), axis=1)
    return (hidden + combined).astype(jnp.bfloat16).reshape(owned_req, num_steps, width)


def solution(mesh):
    return jax.shard_map(
        per_device,
        mesh=mesh,
        in_specs=(
            P("groups", None, "wide"),
            P(("groups", "wide"), None, None),
            P(("groups", "wide"), None, None),
            P(("groups", "wide"), None, None),
            P(("groups", "wide"), None, None),
            P(("groups", "wide"), None, None),
            P(("groups", "wide"), None, None),
            P(("groups", "wide"), None, None),
            P(),
            P("wide", None),
            P(),
            P(),
            P(("groups", "wide"), None, None),
            P("wide", None, None),
            P("wide", None, None),
            P("wide", None, None),
        ),
        out_specs=P(("groups", "wide"), None, None),
        check_vma=False,
    )
```

```python
import functools

import jax
import jax.numpy as jnp
from jax import lax
from jax.experimental import pallas as pl
from jax.experimental.pallas import tpu as pltpu
from jax.sharding import PartitionSpec as P

TOPK = 10
CAP = 2


def unit_rows(vectors):
    vectors = vectors.astype(jnp.float32)
    return vectors * lax.rsqrt(jnp.sum(vectors * vectors, axis=-1, keepdims=True) + 1e-06)


def recurrence(carry_state, q_unit, k_unit, value_cols, beta_cols, decay_cols):
    results = []
    for step_idx in range(q_unit.shape[1]):
        carry_state = carry_state * decay_cols[:, step_idx][:, None]
        key_now = jnp.swapaxes(k_unit[:, step_idx], 1, 2)[..., None]
        predicted = jnp.einsum(
            "bdhc,bhd->bhc", carry_state, k_unit[:, step_idx], precision=lax.Precision.HIGHEST
        )
        change = beta_cols[:, step_idx] * (value_cols[:, step_idx] - predicted)
        carry_state = carry_state + key_now * change[:, None]
        results.append(
            jnp.einsum(
                "bdhc,bhd->bhc", carry_state, q_unit[:, step_idx], precision=lax.Precision.HIGHEST
            )
        )
    return jnp.stack(results, axis=1)


def local_heads(prefill_state, queries, keys_in, values_in, gate_in, beta_rate, decay_rate, norm_gain):
    owned_req, num_steps, _ = queries.shape
    total_req, key_dim, columns = prefill_state.shape
    head_dim = norm_gain.shape[0]
    wide_size = lax.axis_size("wide")
    group = columns // head_dim

    def by_head(array):
        return array.reshape(owned_req, num_steps, wide_size, -1)

    packed = jnp.concatenate(
        [by_head(a) for a in (queries, keys_in, values_in, gate_in, beta_rate, decay_rate)], axis=-1
    )
    got = lax.all_to_all(packed, "wide", split_axis=2, concat_axis=0, tiled=True)[:, :, 0]
    q_raw, k_raw, v_raw, g_raw, beta, decay = jnp.split(
        got,
        [key_dim, 2 * key_dim, 2 * key_dim + columns, 2 * key_dim + 2 * columns, 2 * key_dim + 2 * columns + group],
        axis=-1,
    )

    def inverse_norm(vectors):
        vectors = vectors.astype(jnp.float32)
        return lax.rsqrt(jnp.sum(vectors * vectors, axis=-1) + 1e-06)

    q_inv, k_inv = inverse_norm(q_raw), inverse_norm(k_raw)
    both = jnp.concatenate([k_raw, q_raw], axis=1)
    from_state = jnp.einsum("rsd,rdc->rsc", both, prefill_state, preferred_element_type=jnp.float32)
    gram = jnp.einsum("rsd,rtd->rst", both, k_raw, preferred_element_type=jnp.float32)
    gram = gram * jnp.concatenate([k_inv, q_inv], axis=1)[:, :, None] * k_inv[:, None, :]
    from_state = from_state * jnp.concatenate([k_inv, q_inv], axis=1)[:, :, None]

    def widen(rates):
        return jnp.repeat(rates.astype(jnp.float32), head_dim, axis=-1)

    beta, decay = widen(beta), widen(decay)
    value_cols = v_raw.astype(jnp.float32)
    through = jnp.ones_like(decay[:, 0])
    changes, results = [], []
    for t in range(num_steps):
        through = through * decay[:, t]
        changes = [c * decay[:, t] for c in changes]
        predicted = through * from_state[:, t]
        attended = through * from_state[:, num_steps + t]
        for s, c in enumerate(changes):
            predicted = predicted + gram[:, t, s][:, None] * c
            attended = attended + gram[:, num_steps + t, s][:, None] * c
        now = beta[:, t] * (value_cols[:, t] - predicted)
        attended = attended + gram[:, num_steps + t, t][:, None] * now
        changes.append(now)
        results.append(attended)
    heads_view = jnp.stack(results, axis=1).reshape(total_req * num_steps, group, head_dim)
    scale = lax.rsqrt(jnp.mean(heads_view * heads_view, axis=-1, keepdims=True) + 1e-06)
    gate_act = jax.nn.silu(g_raw.astype(jnp.float32)).reshape(heads_view.shape)
    normed = (heads_view * scale * norm_gain * gate_act).astype(jnp.bfloat16)
    return normed.reshape(total_req * num_steps, columns)


def moved_heads(prefill_state, queries, keys_in, values_in, gate_in, beta_rate, decay_rate, norm_gain):
    wide_size = lax.axis_size("wide")
    owned_req = queries.shape[0]
    num_steps = queries.shape[1]
    local_rows = owned_req * num_steps
    key_dim = prefill_state.shape[1]
    columns = prefill_state.shape[2]
    head_dim = norm_gain.shape[0]
    hv_dv = values_in.shape[2]
    value_heads = hv_dv // head_dim
    key_heads = queries.shape[2] // key_dim
    key_group = hv_dv // key_heads
    arrived = lax.all_to_all(prefill_state, "wide", split_axis=0, concat_axis=2, tiled=True)
    carry_state = arrived.astype(jnp.float32).reshape(owned_req, key_dim, key_heads, key_group)
    q_unit = unit_rows(queries.reshape(owned_req, num_steps, key_heads, key_dim))
    k_unit = unit_rows(keys_in.reshape(owned_req, num_steps, key_heads, key_dim))
    value_cols = values_in.astype(jnp.float32).reshape(owned_req, num_steps, key_heads, key_group)
    beta_cols = jnp.repeat(beta_rate.astype(jnp.float32), head_dim, axis=-1).reshape(
        owned_req, num_steps, key_heads, key_group
    )
    decay_cols = jnp.repeat(decay_rate.astype(jnp.float32), head_dim, axis=-1).reshape(
        owned_req, num_steps, key_heads, key_group
    )
    attended = recurrence(carry_state, q_unit, k_unit, value_cols, beta_cols, decay_cols).reshape(
        local_rows, hv_dv
    )
    heads_view = attended.reshape(local_rows, value_heads, head_dim)
    scale = lax.rsqrt(jnp.mean(heads_view * heads_view, axis=-1, keepdims=True) + 1e-06)
    gate_act = jax.nn.silu(gate_in.reshape(local_rows, value_heads, head_dim).astype(jnp.float32))
    normed = (
        (heads_view * scale * norm_gain * gate_act).astype(jnp.bfloat16).reshape(local_rows, hv_dv)
    )
    return lax.all_to_all(
        normed.reshape(local_rows, wide_size, columns),
        "wide",
        split_axis=1,
        concat_axis=0,
        tiled=True,
    ).reshape(wide_size * local_rows, columns)


def dot(left, right):
    return jnp.dot(left, right, preferred_element_type=jnp.float32)


def dot_nt(left, right):
    return lax.dot_general(
        left, right, (((1,), (1,)), ((), ())), preferred_element_type=jnp.float32
    )


def layer_kernel(
    sizes,
    state_hbm,
    q_ref,
    k_ref,
    v_ref,
    g_ref,
    facts_ref,
    gain_ref,
    out_w_ref,
    resid_ref,
    post_ref,
    router_ref,
    gate_hbm,
    up_hbm,
    down_hbm,
    mixed_ref,
    state,
    outbox,
    inbox,
    from_state,
    heads,
    gate_w,
    up_w,
    down_w,
    core_send,
    core_recv,
    x_send,
    x_recv,
    z_send,
    z_recv,
    part,
    lane_part,
    hidden,
    tokens,
    slab,
    outcome,
    pick_hi,
    pick_lo,
    state_sem,
    box_send_sem,
    box_recv_sem,
    w_sem,
    rs_send_sem,
    rs_recv_sem,
    ag_send_sem,
    ag_recv_sem,
):
    wide_size, owned, width, experts, local_experts, held = sizes
    num_z = wide_size // 4
    rows = wide_size * owned
    half = rows // 2
    me = lax.axis_index("wide")
    core = lax.rem(me, 2)
    x = lax.rem(me // 2, 2)
    z = me // 4

    def device_at(at_z, at_x, at_core):
        return at_z * 4 + at_x * 2 + at_core

    def z_ahead(d):
        return lax.rem(z + d, num_z)

    def z_behind(d):
        return lax.rem(z + num_z - d, num_z)

    core_mate = device_at(z, x, 1 - core)
    x_mate = device_at(z, 1 - x, core)
    z_mates = [device_at(z_ahead(d), x, core) for d in range(1, num_z)]

    def weight_copies(e, slot):
        return [
            pltpu.make_async_copy(hbm.at[e], vmem.at[slot], w_sem.at[i, slot])
            for i, (hbm, vmem) in enumerate(((gate_hbm, gate_w), (up_hbm, up_w), (down_hbm, down_w)))
        ]

    state_copy = pltpu.make_async_copy(state_hbm, state, state_sem)
    state_copy.start()
    for e in range(held):
        for copy in weight_copies(e, e):
            copy.start()

    barrier = pltpu.get_barrier_semaphore()
    moves = [(dz, dx, dc) for dz in range(num_z) for dx in range(2) for dc in range(2)][1:]

    def offset(at_z, dx, dc):
        return device_at(at_z, 1 - x if dx else x, 1 - core if dc else core)

    for dz, dx, dc in moves:
        mate = offset(z_ahead(dz), dx, dc)
        pl.semaphore_signal(
            barrier, inc=1, device_id={"wide": mate}, device_id_type=pl.DeviceIdType.MESH
        )
    requests, num_steps, _ = q_ref.shape

    def flat(ref):
        return jnp.concatenate([ref[r].astype(jnp.float32) for r in range(requests)], axis=0)

    fields = []
    for ref in (q_ref, k_ref, v_ref, g_ref):
        values = flat(ref).astype(jnp.bfloat16)
        size = values.shape[1] // wide_size
        at = sum(fields)
        for to in range(wide_size):
            outbox[to, :, at : at + size] = values[:, to * size : (to + 1) * size]
        fields.append(size)
    key_dim, columns = fields[0], fields[2]
    values_at, gate_at, facts_at = 2 * key_dim, 2 * key_dim + columns, sum(fields)
    for to in range(wide_size):
        outbox[to, :, facts_at:] = facts_ref[...]
    pl.semaphore_wait(barrier, wide_size - 1)

    def remote(src, dst, send_sem, recv_sem, mate):
        return pltpu.make_async_remote_copy(
            src_ref=src,
            dst_ref=dst,
            send_sem=send_sem,
            recv_sem=recv_sem,
            device_id={"wide": mate},
            device_id_type=pl.DeviceIdType.MESH,
        )

    posted = []
    for i in reversed(range(len(moves))):
        dz, dx, dc = moves[i]
        mate = offset(z_ahead(dz), dx, dc)
        copy = remote(
            outbox.at[mate], inbox.at[me], box_send_sem.at[i], box_recv_sem.at[i], mate
        )
        copy.start()
        posted.insert(0, copy)
    inbox[me] = outbox[me]
    state_copy.wait()
    of_request = lax.broadcasted_iota(jnp.int32, (2 * owned, requests * key_dim), 0) % owned
    of_lane = lax.broadcasted_iota(jnp.int32, (2 * owned, requests * key_dim), 1)
    own_state = jnp.where(of_request // num_steps == of_lane // key_dim, 1.0, 0.0)
    own_state = own_state.astype(jnp.bfloat16)

    def meet_state(block):
        came = inbox[block]
        pair = jnp.concatenate([came[:, key_dim : 2 * key_dim], came[:, :key_dim]], axis=0)
        spaced = jnp.concatenate([pair] * requests, axis=1) * own_state
        from_state[block] = dot(spaced, state[block])

    meet_state(me)
    for i, (dz, dx, dc) in enumerate(moves):
        posted[i].wait_recv()
        meet_state(offset(z_behind(dz), dx, dc))

    at_once = 4
    many = at_once * owned
    head_dim = gain_ref.shape[1]
    group = columns // head_dim
    value_heads = group * wide_size
    step = lax.broadcasted_iota(jnp.int32, (many, head_dim), 0) % num_steps
    step_col = step[:, :1]
    lane = lax.broadcasted_iota(jnp.int32, (many, 128), 1)

    def unit(vectors):
        return lax.rsqrt(jnp.sum(vectors * vectors, axis=1, keepdims=True) + 1e-06)

    def before(array, d):
        return pltpu.roll(array, d, 0) if d else array

    for first in range(0, wide_size, at_once):
        came = inbox[first : first + at_once].reshape(many, inbox.shape[-1])
        q_raw = came[:, :key_dim].astype(jnp.float32)
        k_raw = came[:, key_dim : 2 * key_dim].astype(jnp.float32)
        q_inv, k_inv = unit(q_raw), unit(k_raw)
        q_unit, k_unit = q_raw * q_inv, k_raw * k_inv
        met = from_state[first : first + at_once]
        k_met = met[:, :owned].reshape(many, columns) * k_inv
        q_met = met[:, owned:].reshape(many, columns) * q_inv
        kk, qk = [], []
        for d in range(num_steps):
            earlier = before(k_unit, d)
            valid = step_col >= d
            kk.append(
                jnp.where(valid, jnp.sum(k_unit * earlier, axis=1, keepdims=True), 0.0)
            )
            qk.append(
                jnp.where(valid, jnp.sum(q_unit * earlier, axis=1, keepdims=True), 0.0)
            )
        facts = came[:, facts_at:].astype(jnp.float32)
        for j in range(group):
            cut = slice(j * head_dim, (j + 1) * head_dim)
            head = me * group + j
            beta = jnp.sum(jnp.where(lane == head, facts, 0.0), axis=1, keepdims=True)
            decay = jnp.sum(
                jnp.where(lane == head + value_heads, facts, 0.0), axis=1, keepdims=True
            )
            decay = jnp.broadcast_to(decay, (many, head_dim))
            kept = [None, decay]
            for d in range(1, num_steps):
                kept.append(kept[d] * before(decay, d))
            through = decay
            for t in range(1, num_steps):
                through = jnp.where(step == t, kept[t + 1], through)
            value_cols = came[:, values_at:gate_at][:, cut].astype(jnp.float32)
            base = value_cols - through * k_met[:, cut]
            change = beta * base
            for _ in range(1, num_steps):
                rest = base
                for d in range(1, num_steps):
                    rest = rest - kept[d] * kk[d] * before(change, d)
                change = beta * rest
            attended = through * q_met[:, cut] + qk[0] * change
            for d in range(1, num_steps):
                attended = attended + kept[d] * qk[d] * before(change, d)
            scale = lax.rsqrt(jnp.mean(attended * attended, axis=1, keepdims=True) + 1e-06)
            gate_act = jax.nn.silu(came[:, gate_at:facts_at][:, cut].astype(jnp.float32))
            normed = (attended * scale * gain_ref[...] * gate_act).astype(jnp.bfloat16)
            heads[first // 2 : (first + at_once) // 2, :, :, cut] = normed.reshape(
                at_once // 2, 2, owned, head_dim
            )

    def reduce_scatter(turn, produce):
        def exchange(i, src, dst, mate):
            copy = remote(src, dst, rs_send_sem.at[turn, i], rs_recv_sem.at[turn, i], mate)
            copy.start()
            return copy

        core_send[turn] = produce(1 - core).astype(jnp.bfloat16).reshape(num_z, 2, owned, width)
        to_core = exchange(0, core_send.at[turn], core_recv.at[turn], core_mate)
        part[...] = produce(core).reshape(num_z, 2, owned, width)
        to_core.wait()
        x_send[turn] = (part[:, 1 - x] + core_recv[turn, :, 1 - x].astype(jnp.float32)).astype(
            jnp.bfloat16
        )
        to_x = exchange(1, x_send.at[turn], x_recv.at[turn], x_mate)
        lane_part[...] = part[:, x] + core_recv[turn, :, x].astype(jnp.float32)
        to_x.wait()
        to_z = []
        for d in range(1, num_z):
            at_z = z_ahead(d)
            z_send[turn, d - 1] = (
                lane_part[at_z] + x_recv[turn, at_z].astype(jnp.float32)
            ).astype(jnp.bfloat16)
            to_z.append(
                exchange(1 + d, z_send.at[turn, d - 1], z_recv.at[turn, d - 1], z_mates[d - 1])
            )
        total = lane_part[z] + x_recv[turn, z].astype(jnp.float32)
        for d in range(1, num_z):
            to_z[d - 1].wait()
            total = total + z_recv[turn, d - 1].astype(jnp.float32)
        return total

    def project(at_core):
        return dot(heads[:, at_core].reshape(half, columns), out_w_ref[...])

    now = flat(resid_ref) + reduce_scatter(0, project)
    hidden[...] = now
    moe_in = now * lax.rsqrt(jnp.mean(now * now, axis=-1, keepdims=True) + 1e-06) * post_ref[...]
    tokens[me] = moe_in.astype(jnp.bfloat16)

    sent = []

    def pass_on(block, mate):
        copy = remote(
            tokens.at[block],
            tokens.at[block],
            ag_send_sem.at[len(sent)],
            ag_recv_sem.at[block],
            mate,
        )
        copy.start()
        sent.append(copy)

    def arrived(block, mate):
        remote(
            tokens.at[block], tokens.at[block], ag_send_sem.at[0], ag_recv_sem.at[block], mate
        ).wait_recv()

    for mate in z_mates:
        pass_on(me, mate)
    pass_on(me, x_mate)
    pass_on(me, core_mate)
    arrived(x_mate, x_mate)
    pass_on(x_mate, core_mate)
    for d in range(1, num_z):
        block = device_at(z_behind(d), x, core)
        arrived(block, x_mate)
        pass_on(block, x_mate)
        pass_on(block, core_mate)
    for d in range(1, num_z):
        block = device_at(z_behind(d), 1 - x, core)
        arrived(block, x_mate)
        pass_on(block, core_mate)
    for at_z in range(num_z):
        for at_x in range(2):
            arrived(device_at(at_z, at_x, 1 - core), core_mate)
    for copy in posted + sent:
        copy.wait_send()

    all_in = tokens[...].reshape(rows, width)
    named = inbox[:, :, facts_at:].reshape(rows, 128).astype(jnp.float32)
    logits = dot(all_in, router_ref[...])
    lanes = lax.broadcasted_iota(jnp.int32, (rows, experts), 1).astype(jnp.float32)
    squashed = jnp.zeros((rows, experts), jnp.float32)
    chosen = jnp.zeros((rows, experts), jnp.float32)
    ids_at = 2 * value_heads
    for k in range(TOPK):
        chosen = jnp.where(named[:, ids_at + k : ids_at + k + 1] == lanes, 1.0, chosen)
    squashed = jnp.where(chosen > 0.5, jax.nn.sigmoid(logits), 0.0)
    gates = squashed / jnp.sum(squashed, axis=1, keepdims=True)
    gates_hi = gates.astype(jnp.bfloat16)
    gates_lo = (gates - gates_hi.astype(jnp.float32)).astype(jnp.bfloat16)
    mine = (
        lax.broadcasted_iota(jnp.int32, (local_experts, experts), 1)
        == lax.broadcasted_iota(jnp.int32, (local_experts, experts), 0) + me * local_experts
    )
    mine = jnp.where(mine, 1.0, 0.0).astype(jnp.bfloat16)
    hits = dot_nt(mine, chosen.astype(jnp.bfloat16))
    local_hi = dot_nt(mine, gates_hi)
    local_lo = dot_nt(mine, gates_lo)
    row_a = lax.broadcasted_iota(jnp.int32, (rows, rows), 0)
    row_b = lax.broadcasted_iota(jnp.int32, (rows, rows), 1)
    earlier = (row_a // owned == row_b // owned) & (row_a < row_b)
    rank = dot(hits.astype(jnp.bfloat16), jnp.where(earlier, 1.0, 0.0).astype(jnp.bfloat16))
    origin = lax.broadcasted_iota(jnp.int32, (local_experts, rows), 1) // owned
    place = jnp.where(hits > 0.5, (origin * CAP).astype(jnp.float32) + rank, -1.0)
    slots = CAP * wide_size
    slot_no = lax.broadcasted_iota(jnp.int32, (slots, rows), 0).astype(jnp.float32)
    takes, takes_hi, takes_lo = [], [], []
    for e in range(local_experts):
        taken = place[e : e + 1] == slot_no
        takes.append(jnp.where(taken, 1.0, 0.0))
        takes_hi.append(jnp.where(taken, local_hi[e : e + 1], 0.0))
        takes_lo.append(jnp.where(taken, local_lo[e : e + 1], 0.0))
    take = jnp.concatenate(takes, axis=0).astype(jnp.bfloat16)
    slab[...] = dot(take, all_in).astype(jnp.bfloat16).reshape(local_experts, slots, width)

    def back(pieces):
        turned = jnp.concatenate(pieces, axis=0).T.astype(jnp.bfloat16)
        return turned.reshape(num_z * 2, 2, owned, local_experts * slots)

    pick_hi[...] = back(takes_hi)
    pick_lo[...] = back(takes_lo)

    @pl.loop(0, local_experts)
    def _(e):
        slot = lax.rem(e, held)
        for copy in weight_copies(e, slot):
            copy.wait()
        came = slab[e]
        gate_part = dot(came, gate_w[slot])
        up_part = dot(came, up_w[slot])
        mid = (jax.nn.silu(gate_part) * up_part).astype(jnp.bfloat16)
        outcome[e] = dot(mid, down_w[slot]).astype(jnp.bfloat16)

        @pl.when(e + held < local_experts)
        def _():
            for copy in weight_copies(e + held, slot):
                copy.start()

    def combine(at_core):
        results = outcome[...].reshape(local_experts * slots, width)
        hi = pick_hi[:, at_core].reshape(half, local_experts * slots)
        lo = pick_lo[:, at_core].reshape(half, local_experts * slots)
        return dot(hi, results) + dot(lo, results)

    result = reduce_scatter(1, combine) + hidden[...]
    for r in range(requests):
        mixed_ref[r] = result[r * num_steps : (r + 1) * num_steps].astype(mixed_ref.dtype)


def fused_layer(
    prefill_state,
    residual_in,
    queries,
    keys_in,
    values_in,
    gate_in,
    beta_rate,
    decay_rate,
    norm_gain,
    out_weight,
    post_gain,
    router_weight,
    expert_ids,
    expert_gate,
    expert_up,
    expert_down,
):
    wide_size = lax.axis_size("wide")
    owned_req, num_steps, width = residual_in.shape
    owned = owned_req * num_steps
    rows = wide_size * owned
    total_req, key_dim, columns = prefill_state.shape
    value_heads = beta_rate.shape[2]
    box = 2 * key_dim + 2 * columns + 128
    num_z = wide_size // 4
    experts = router_weight.shape[1]
    local_experts, _, hidden_units = expert_gate.shape
    held = min(local_experts, 6)
    slots = CAP * wide_size
    facts = jnp.concatenate(
        [beta_rate, decay_rate, expert_ids.astype(jnp.bfloat16)], axis=-1
    ).reshape(owned, 2 * value_heads + TOPK)
    facts = jnp.pad(facts, ((0, 0), (0, 128 - facts.shape[1])))
    half16 = (2, num_z, 2, owned, width)
    bf16, f32 = jnp.bfloat16, jnp.float32
    vmem = pl.BlockSpec(memory_space=pltpu.VMEM)
    hbm = pl.BlockSpec(memory_space=pl.ANY)
    out = pl.pallas_call(
        functools.partial(
            layer_kernel, (wide_size, owned, width, experts, local_experts, held)
        ),
        out_shape=jax.ShapeDtypeStruct((owned_req, num_steps, width), bf16),
        in_specs=[hbm] + [vmem] * 10 + [hbm] * 3,
        out_specs=vmem,
        scratch_shapes=[
            pltpu.VMEM((wide_size, owned_req * key_dim, columns), bf16),
            pltpu.VMEM((wide_size, owned, box), bf16),
            pltpu.VMEM((wide_size, owned, box), bf16),
            pltpu.VMEM((wide_size, 2 * owned, columns), f32),
            pltpu.VMEM((num_z * 2, 2, owned, columns), bf16),
            pltpu.VMEM((held, width, hidden_units), bf16),
            pltpu.VMEM((held, width, hidden_units), bf16),
            pltpu.VMEM((held, hidden_units, width), bf16),
            pltpu.VMEM(half16, bf16),
            pltpu.VMEM(half16, bf16),
            pltpu.VMEM((2, num_z, owned, width), bf16),
            pltpu.VMEM((2, num_z, owned, width), bf16),
            pltpu.VMEM((2, num_z - 1, owned, width), bf16),
            pltpu.VMEM((2, num_z - 1, owned, width), bf16),
            pltpu.VMEM((num_z, 2, owned, width), f32),
            pltpu.VMEM((num_z, owned, width), f32),
            pltpu.VMEM((owned, width), f32),
            pltpu.VMEM((wide_size, owned, width), bf16),
            pltpu.VMEM((local_experts, slots, width), bf16),
            pltpu.VMEM((local_experts, slots, width), bf16),
            pltpu.VMEM((num_z * 2, 2, owned, local_experts * slots), bf16),
            pltpu.VMEM((num_z * 2, 2, owned, local_experts * slots), bf16),
            pltpu.SemaphoreType.DMA,
            pltpu.SemaphoreType.DMA((wide_size - 1,)),
            pltpu.SemaphoreType.DMA((wide_size - 1,)),
            pltpu.SemaphoreType.DMA((3, held)),
            pltpu.SemaphoreType.DMA((2, 1 + num_z)),
            pltpu.SemaphoreType.DMA((2, 1 + num_z)),
            pltpu.SemaphoreType.DMA((wide_size,)),
            pltpu.SemaphoreType.DMA((wide_size,)),
        ],
        compiler_params=pltpu.CompilerParams(
            collective_id=0, has_side_effects=True, vmem_limit_bytes=60 * 1024 * 1024
        ),
    )(
        prefill_state.reshape(wide_size, owned_req * key_dim, columns),
        queries,
        keys_in,
        values_in,
        gate_in,
        facts,
        norm_gain.reshape(1, norm_gain.shape[0]),
        out_weight,
        residual_in,
        post_gain.reshape(1, width),
        router_weight,
        expert_gate,
        expert_up,
        expert_down,
    )
    return out


def per_device(
    prefill_state,
    residual_in,
    queries,
    keys_in,
    values_in,
    gate_in,
    beta_rate,
    decay_rate,
    norm_gain,
    out_weight,
    post_gain,
    router_weight,
    expert_ids,
    expert_gate,
    expert_up,
    expert_down,
):
    wide_size = lax.axis_size("wide")
    owned_req = queries.shape[0]
    num_steps = queries.shape[1]
    local_rows = owned_req * num_steps
    key_dim = prefill_state.shape[1]
    columns = prefill_state.shape[2]
    head_dim = norm_gain.shape[0]
    hv_dv = values_in.shape[2]
    value_heads = hv_dv // head_dim
    key_heads = queries.shape[2] // key_dim
    key_group = hv_dv // key_heads
    width = residual_in.shape[2]
    if key_heads == wide_size == 16 and local_rows == 16 and router_weight.shape[1] == 128:
        return fused_layer(
            prefill_state,
            residual_in,
            queries,
            keys_in,
            values_in,
            gate_in,
            beta_rate,
            decay_rate,
            norm_gain,
            out_weight,
            post_gain,
            router_weight,
            expert_ids,
            expert_gate,
            expert_up,
            expert_down,
        )
    heads = local_heads if key_heads == wide_size else moved_heads
    spread = heads(
        prefill_state, queries, keys_in, values_in, gate_in, beta_rate, decay_rate, norm_gain
    )
    attention = lax.psum_scatter(
        jnp.dot(spread, out_weight, preferred_element_type=jnp.float32),
        "wide",
        scatter_dimension=0,
        tiled=True,
    )
    hidden = residual_in.reshape(local_rows, width).astype(jnp.float32) + attention
    moe_in = (
        hidden * lax.rsqrt(jnp.mean(hidden * hidden, axis=-1, keepdims=True) + 1e-06) * post_gain
    ).astype(jnp.bfloat16)
    logits = jnp.dot(moe_in, router_weight, preferred_element_type=jnp.float32)
    num_experts = router_weight.shape[1]
    flat_ids = expert_ids.reshape(local_rows, TOPK)
    onehot = flat_ids[:, :, None] == jnp.arange(num_experts, dtype=jnp.int32)[None, None, :]
    chosen = jnp.sum(jnp.where(onehot, logits[:, None, :], 0.0), axis=-1)
    squashed = jax.nn.sigmoid(chosen)
    gates = squashed / jnp.sum(squashed, axis=1, keepdims=True)
    counts_flat = onehot.reshape(local_rows * TOPK, num_experts).astype(jnp.int32)
    running = jnp.cumsum(counts_flat, axis=0) - 1
    slot_of = jnp.sum(counts_flat * running, axis=1).reshape(local_rows, TOPK)
    position = flat_ids * CAP + slot_of
    dispatch = jnp.any(
        position[:, :, None] == jnp.arange(num_experts * CAP, dtype=jnp.int32)[None, None, :],
        axis=1,
    ).astype(jnp.bfloat16)
    buffer = jnp.einsum("rs,rd->sd", dispatch, moe_in, preferred_element_type=jnp.float32).astype(
        jnp.bfloat16
    )
    exp_dev = expert_gate.shape[0]
    buffer = buffer.reshape(wide_size, exp_dev, CAP, width)
    slab_in = lax.all_to_all(buffer, "wide", split_axis=0, concat_axis=0, tiled=True)
    gate_part = jnp.einsum(
        "sekd,edf->sekf", slab_in, expert_gate, preferred_element_type=jnp.float32
    )
    up_part = jnp.einsum("sekd,edf->sekf", slab_in, expert_up, preferred_element_type=jnp.float32)
    hidden_mid = (jax.nn.silu(gate_part) * up_part).astype(jnp.bfloat16)
    processed = jnp.einsum(
        "sekf,efd->sekd", hidden_mid, expert_down, preferred_element_type=jnp.float32
    ).astype(jnp.bfloat16)
    returned = lax.all_to_all(processed, "wide", split_axis=0, concat_axis=0, tiled=True).reshape(
        num_experts * CAP, width
    )
    picked = returned[position]
    combined = jnp.sum(gates[:, :, None] * picked.astype(jnp.float32), axis=1)
    return (hidden + combined).astype(jnp.bfloat16).reshape(owned_req, num_steps, width)


def solution(mesh):
    return jax.shard_map(
        per_device,
        mesh=mesh,
        in_specs=(
            P("groups", None, "wide"),
            P(("groups", "wide"), None, None),
            P(("groups", "wide"), None, None),
            P(("groups", "wide"), None, None),
            P(("groups", "wide"), None, None),
            P(("groups", "wide"), None, None),
            P(("groups", "wide"), None, None),
            P(("groups", "wide"), None, None),
            P(),
            P("wide", None),
            P(),
            P(),
            P(("groups", "wide"), None, None),
            P("wide", None, None),
            P("wide", None, None),
            P("wide", None, None),
        ),
        out_specs=P(("groups", "wide"), None, None),
        check_vma=False,
    )
```

```python
import functools

import jax
import jax.numpy as jnp
from jax import lax
from jax.experimental import pallas as pl
from jax.experimental.pallas import tpu as pltpu
from jax.sharding import PartitionSpec as P

TOPK = 10
CAP = 2


def unit_rows(vectors):
    vectors = vectors.astype(jnp.float32)
    return vectors * lax.rsqrt(jnp.sum(vectors * vectors, axis=-1, keepdims=True) + 1e-06)


def recurrence(carry_state, q_unit, k_unit, value_cols, beta_cols, decay_cols):
    results = []
    for step_idx in range(q_unit.shape[1]):
        carry_state = carry_state * decay_cols[:, step_idx][:, None]
        key_now = jnp.swapaxes(k_unit[:, step_idx], 1, 2)[..., None]
        predicted = jnp.einsum(
            "bdhc,bhd->bhc", carry_state, k_unit[:, step_idx], precision=lax.Precision.HIGHEST
        )
        change = beta_cols[:, step_idx] * (value_cols[:, step_idx] - predicted)
        carry_state = carry_state + key_now * change[:, None]
        results.append(
            jnp.einsum(
                "bdhc,bhd->bhc", carry_state, q_unit[:, step_idx], precision=lax.Precision.HIGHEST
            )
        )
    return jnp.stack(results, axis=1)


def local_heads(prefill_state, queries, keys_in, values_in, gate_in, beta_rate, decay_rate, norm_gain):
    owned_req, num_steps, _ = queries.shape
    total_req, key_dim, columns = prefill_state.shape
    head_dim = norm_gain.shape[0]
    wide_size = lax.axis_size("wide")
    group = columns // head_dim

    def by_head(array):
        return array.reshape(owned_req, num_steps, wide_size, -1)

    packed = jnp.concatenate(
        [by_head(a) for a in (queries, keys_in, values_in, gate_in, beta_rate, decay_rate)], axis=-1
    )
    got = lax.all_to_all(packed, "wide", split_axis=2, concat_axis=0, tiled=True)[:, :, 0]
    q_raw, k_raw, v_raw, g_raw, beta, decay = jnp.split(
        got,
        [key_dim, 2 * key_dim, 2 * key_dim + columns, 2 * key_dim + 2 * columns, 2 * key_dim + 2 * columns + group],
        axis=-1,
    )

    def inverse_norm(vectors):
        vectors = vectors.astype(jnp.float32)
        return lax.rsqrt(jnp.sum(vectors * vectors, axis=-1) + 1e-06)

    q_inv, k_inv = inverse_norm(q_raw), inverse_norm(k_raw)
    both = jnp.concatenate([k_raw, q_raw], axis=1)
    from_state = jnp.einsum("rsd,rdc->rsc", both, prefill_state, preferred_element_type=jnp.float32)
    gram = jnp.einsum("rsd,rtd->rst", both, k_raw, preferred_element_type=jnp.float32)
    gram = gram * jnp.concatenate([k_inv, q_inv], axis=1)[:, :, None] * k_inv[:, None, :]
    from_state = from_state * jnp.concatenate([k_inv, q_inv], axis=1)[:, :, None]

    def widen(rates):
        return jnp.repeat(rates.astype(jnp.float32), head_dim, axis=-1)

    beta, decay = widen(beta), widen(decay)
    value_cols = v_raw.astype(jnp.float32)
    through = jnp.ones_like(decay[:, 0])
    changes, results = [], []
    for t in range(num_steps):
        through = through * decay[:, t]
        changes = [c * decay[:, t] for c in changes]
        predicted = through * from_state[:, t]
        attended = through * from_state[:, num_steps + t]
        for s, c in enumerate(changes):
            predicted = predicted + gram[:, t, s][:, None] * c
            attended = attended + gram[:, num_steps + t, s][:, None] * c
        now = beta[:, t] * (value_cols[:, t] - predicted)
        attended = attended + gram[:, num_steps + t, t][:, None] * now
        changes.append(now)
        results.append(attended)
    heads_view = jnp.stack(results, axis=1).reshape(total_req * num_steps, group, head_dim)
    scale = lax.rsqrt(jnp.mean(heads_view * heads_view, axis=-1, keepdims=True) + 1e-06)
    gate_act = jax.nn.silu(g_raw.astype(jnp.float32)).reshape(heads_view.shape)
    normed = (heads_view * scale * norm_gain * gate_act).astype(jnp.bfloat16)
    return normed.reshape(total_req * num_steps, columns)


def moved_heads(prefill_state, queries, keys_in, values_in, gate_in, beta_rate, decay_rate, norm_gain):
    wide_size = lax.axis_size("wide")
    owned_req = queries.shape[0]
    num_steps = queries.shape[1]
    local_rows = owned_req * num_steps
    key_dim = prefill_state.shape[1]
    columns = prefill_state.shape[2]
    head_dim = norm_gain.shape[0]
    hv_dv = values_in.shape[2]
    value_heads = hv_dv // head_dim
    key_heads = queries.shape[2] // key_dim
    key_group = hv_dv // key_heads
    arrived = lax.all_to_all(prefill_state, "wide", split_axis=0, concat_axis=2, tiled=True)
    carry_state = arrived.astype(jnp.float32).reshape(owned_req, key_dim, key_heads, key_group)
    q_unit = unit_rows(queries.reshape(owned_req, num_steps, key_heads, key_dim))
    k_unit = unit_rows(keys_in.reshape(owned_req, num_steps, key_heads, key_dim))
    value_cols = values_in.astype(jnp.float32).reshape(owned_req, num_steps, key_heads, key_group)
    beta_cols = jnp.repeat(beta_rate.astype(jnp.float32), head_dim, axis=-1).reshape(
        owned_req, num_steps, key_heads, key_group
    )
    decay_cols = jnp.repeat(decay_rate.astype(jnp.float32), head_dim, axis=-1).reshape(
        owned_req, num_steps, key_heads, key_group
    )
    attended = recurrence(carry_state, q_unit, k_unit, value_cols, beta_cols, decay_cols).reshape(
        local_rows, hv_dv
    )
    heads_view = attended.reshape(local_rows, value_heads, head_dim)
    scale = lax.rsqrt(jnp.mean(heads_view * heads_view, axis=-1, keepdims=True) + 1e-06)
    gate_act = jax.nn.silu(gate_in.reshape(local_rows, value_heads, head_dim).astype(jnp.float32))
    normed = (
        (heads_view * scale * norm_gain * gate_act).astype(jnp.bfloat16).reshape(local_rows, hv_dv)
    )
    return lax.all_to_all(
        normed.reshape(local_rows, wide_size, columns),
        "wide",
        split_axis=1,
        concat_axis=0,
        tiled=True,
    ).reshape(wide_size * local_rows, columns)


def dot(left, right):
    return jnp.dot(left, right, preferred_element_type=jnp.float32)


def dot_nt(left, right):
    return lax.dot_general(
        left, right, (((1,), (1,)), ((), ())), preferred_element_type=jnp.float32
    )


def layer_kernel(
    sizes,
    state_hbm,
    q_ref,
    k_ref,
    v_ref,
    g_ref,
    facts_ref,
    gain_ref,
    out_w_ref,
    resid_ref,
    post_ref,
    router_ref,
    gate_hbm,
    up_hbm,
    down_hbm,
    mixed_ref,
    state,
    outbox,
    inbox,
    from_state,
    heads,
    gate_w,
    up_w,
    down_w,
    core_send,
    core_recv,
    x_send,
    x_recv,
    z_send,
    z_recv,
    part,
    lane_part,
    hidden,
    tokens,
    slab,
    mid,
    pick_hi,
    pick_lo,
    state_sem,
    box_send_sem,
    box_recv_sem,
    w_sem,
    down_sem,
    rs_send_sem,
    rs_recv_sem,
    ag_send_sem,
    ag_recv_sem,
):
    wide_size, owned, width, experts, local_experts, held, chunks = sizes
    num_z = wide_size // 4
    rows = wide_size * owned
    half = rows // 2
    me = lax.axis_index("wide")
    core = lax.rem(me, 2)
    x = lax.rem(me // 2, 2)
    z = me // 4

    def device_at(at_z, at_x, at_core):
        return at_z * 4 + at_x * 2 + at_core

    def z_ahead(d):
        return lax.rem(z + d, num_z)

    def z_behind(d):
        return lax.rem(z + num_z - d, num_z)

    core_mate = device_at(z, x, 1 - core)
    x_mate = device_at(z, 1 - x, core)
    z_mates = [device_at(z_ahead(d), x, core) for d in range(1, num_z)]

    def up_copies(e, slot):
        return [
            pltpu.make_async_copy(hbm.at[e], vmem.at[slot], w_sem.at[i, slot])
            for i, (hbm, vmem) in enumerate(((gate_hbm, gate_w), (up_hbm, up_w)))
        ]

    def down_copy(e):
        return pltpu.make_async_copy(down_hbm.at[e], down_w.at[e], down_sem.at[e])

    state_copy = pltpu.make_async_copy(state_hbm, state, state_sem)
    state_copy.start()
    barrier = pltpu.get_barrier_semaphore()
    moves = [(dz, dx, dc) for dz in range(num_z) for dx in range(2) for dc in range(2)][1:]

    def offset(at_z, dx, dc):
        return device_at(at_z, 1 - x if dx else x, 1 - core if dc else core)

    for dz, dx, dc in moves:
        mate = offset(z_ahead(dz), dx, dc)
        pl.semaphore_signal(
            barrier, inc=1, device_id={"wide": mate}, device_id_type=pl.DeviceIdType.MESH
        )
    requests, num_steps, _ = q_ref.shape

    def flat(ref):
        return jnp.concatenate([ref[r].astype(jnp.float32) for r in range(requests)], axis=0)

    fields = []
    for ref in (q_ref, k_ref, v_ref, g_ref):
        values = flat(ref).astype(jnp.bfloat16)
        size = values.shape[1] // wide_size
        at = sum(fields)
        for to in range(wide_size):
            outbox[to, :, at : at + size] = values[:, to * size : (to + 1) * size]
        fields.append(size)
    key_dim, columns = fields[0], fields[2]
    values_at, gate_at, facts_at = 2 * key_dim, 2 * key_dim + columns, sum(fields)
    for to in range(wide_size):
        outbox[to, :, facts_at:] = facts_ref[...]
    pl.semaphore_wait(barrier, wide_size - 1)

    def remote(src, dst, send_sem, recv_sem, mate):
        return pltpu.make_async_remote_copy(
            src_ref=src,
            dst_ref=dst,
            send_sem=send_sem,
            recv_sem=recv_sem,
            device_id={"wide": mate},
            device_id_type=pl.DeviceIdType.MESH,
        )

    posted = []
    for i in reversed(range(len(moves))):
        dz, dx, dc = moves[i]
        mate = offset(z_ahead(dz), dx, dc)
        copy = remote(
            outbox.at[mate], inbox.at[me], box_send_sem.at[i], box_recv_sem.at[i], mate
        )
        copy.start()
        posted.insert(0, copy)
    inbox[me] = outbox[me]
    state_copy.wait()
    of_request = lax.broadcasted_iota(jnp.int32, (2 * owned, requests * key_dim), 0) % owned
    of_lane = lax.broadcasted_iota(jnp.int32, (2 * owned, requests * key_dim), 1)
    own_state = jnp.where(of_request // num_steps == of_lane // key_dim, 1.0, 0.0)
    own_state = own_state.astype(jnp.bfloat16)

    def meet_state(block):
        came = inbox[block]
        pair = jnp.concatenate([came[:, key_dim : 2 * key_dim], came[:, :key_dim]], axis=0)
        spaced = jnp.concatenate([pair] * requests, axis=1) * own_state
        from_state[block] = dot(spaced, state[block])

    meet_state(me)
    for i, (dz, dx, dc) in enumerate(moves):
        posted[i].wait_recv()
        meet_state(offset(z_behind(dz), dx, dc))

    for e in range(held):
        for copy in up_copies(e, e):
            copy.start()
    for e in range(local_experts):
        down_copy(e).start()

    at_once = 4
    many = at_once * owned
    head_dim = gain_ref.shape[1]
    group = columns // head_dim
    value_heads = group * wide_size
    step = lax.broadcasted_iota(jnp.int32, (many, head_dim), 0) % num_steps
    step_col = step[:, :1]
    lane = lax.broadcasted_iota(jnp.int32, (many, 128), 1)

    def unit(vectors):
        return lax.rsqrt(jnp.sum(vectors * vectors, axis=1, keepdims=True) + 1e-06)

    def before(array, d):
        return pltpu.roll(array, d, 0) if d else array

    for first in range(0, wide_size, at_once):
        came = inbox[first : first + at_once].reshape(many, inbox.shape[-1])
        q_raw = came[:, :key_dim].astype(jnp.float32)
        k_raw = came[:, key_dim : 2 * key_dim].astype(jnp.float32)
        q_inv, k_inv = unit(q_raw), unit(k_raw)
        q_unit, k_unit = q_raw * q_inv, k_raw * k_inv
        met = from_state[first : first + at_once]
        k_met = met[:, :owned].reshape(many, columns) * k_inv
        q_met = met[:, owned:].reshape(many, columns) * q_inv
        kk, qk = [], []
        for d in range(num_steps):
            earlier = before(k_unit, d)
            valid = step_col >= d
            kk.append(
                jnp.where(valid, jnp.sum(k_unit * earlier, axis=1, keepdims=True), 0.0)
            )
            qk.append(
                jnp.where(valid, jnp.sum(q_unit * earlier, axis=1, keepdims=True), 0.0)
            )
        facts = came[:, facts_at:].astype(jnp.float32)
        for j in range(group):
            cut = slice(j * head_dim, (j + 1) * head_dim)
            head = me * group + j
            beta = jnp.sum(jnp.where(lane == head, facts, 0.0), axis=1, keepdims=True)
            decay = jnp.sum(
                jnp.where(lane == head + value_heads, facts, 0.0), axis=1, keepdims=True
            )
            decay = jnp.broadcast_to(decay, (many, head_dim))
            kept = [None, decay]
            for d in range(1, num_steps):
                kept.append(kept[d] * before(decay, d))
            through = decay
            for t in range(1, num_steps):
                through = jnp.where(step == t, kept[t + 1], through)
            value_cols = came[:, values_at:gate_at][:, cut].astype(jnp.float32)
            base = value_cols - through * k_met[:, cut]
            change = beta * base
            for _ in range(1, num_steps):
                rest = base
                for d in range(1, num_steps):
                    rest = rest - kept[d] * kk[d] * before(change, d)
                change = beta * rest
            attended = through * q_met[:, cut] + qk[0] * change
            for d in range(1, num_steps):
                attended = attended + kept[d] * qk[d] * before(change, d)
            scale = lax.rsqrt(jnp.mean(attended * attended, axis=1, keepdims=True) + 1e-06)
            gate_act = jax.nn.silu(came[:, gate_at:facts_at][:, cut].astype(jnp.float32))
            normed = (attended * scale * gain_ref[...] * gate_act).astype(jnp.bfloat16)
            heads[first // 2 : (first + at_once) // 2, :, :, cut] = normed.reshape(
                at_once // 2, 2, owned, head_dim
            )

    wide_cut = width // chunks

    def reduce_scatter(turn, produce):
        started = {}

        def exchange(c, i, src, dst, mate):
            copy = remote(src, dst, rs_send_sem.at[turn, c, i], rs_recv_sem.at[turn, c, i], mate)
            copy.start()
            started[c, i] = copy

        def over_cores(c):
            sums = produce(c)
            core_send[turn, c] = (
                sums(1 - core).astype(jnp.bfloat16).reshape(num_z, 2, owned, wide_cut)
            )
            exchange(c, 0, core_send.at[turn, c], core_recv.at[turn, c], core_mate)
            part[c] = sums(core).reshape(num_z, 2, owned, wide_cut)

        def over_x(c):
            started[c, 0].wait_recv()
            x_send[turn, c] = (
                part[c, :, 1 - x] + core_recv[turn, c, :, 1 - x].astype(jnp.float32)
            ).astype(jnp.bfloat16)
            exchange(c, 1, x_send.at[turn, c], x_recv.at[turn, c], x_mate)
            lane_part[c] = part[c, :, x] + core_recv[turn, c, :, x].astype(jnp.float32)

        def over_z(c):
            started[c, 1].wait_recv()
            for d in range(1, num_z):
                at_z = z_ahead(d)
                z_send[turn, c, d - 1] = (
                    lane_part[c, at_z] + x_recv[turn, c, at_z].astype(jnp.float32)
                ).astype(jnp.bfloat16)
                exchange(
                    c, 1 + d, z_send.at[turn, c, d - 1], z_recv.at[turn, c, d - 1], z_mates[d - 1]
                )

        def total(c):
            value = lane_part[c, z] + x_recv[turn, c, z].astype(jnp.float32)
            for d in range(1, num_z):
                started[c, 1 + d].wait_recv()
                value = value + z_recv[turn, c, d - 1].astype(jnp.float32)
            return value

        totals = []
        for tick in range(chunks + 3):
            for late, stage in enumerate((over_cores, over_x, over_z)):
                if 0 <= tick - late < chunks:
                    stage(tick - late)
            if tick >= 3:
                totals.append(total(tick - 3))
        for copy in started.values():
            copy.wait_send()
        return jnp.concatenate(totals, axis=1)

    def project(c):
        weights = out_w_ref[:, c * wide_cut : (c + 1) * wide_cut]
        return lambda at_core: dot(heads[:, at_core].reshape(half, columns), weights)

    now = flat(resid_ref) + reduce_scatter(0, project)
    hidden[...] = now
    moe_in = now * lax.rsqrt(jnp.mean(now * now, axis=-1, keepdims=True) + 1e-06) * post_ref[...]
    tokens[me] = moe_in.astype(jnp.bfloat16)

    sent = []

    def pass_on(block, mate):
        copy = remote(
            tokens.at[block],
            tokens.at[block],
            ag_send_sem.at[len(sent)],
            ag_recv_sem.at[block],
            mate,
        )
        copy.start()
        sent.append(copy)

    def arrived(block, mate):
        remote(
            tokens.at[block], tokens.at[block], ag_send_sem.at[0], ag_recv_sem.at[block], mate
        ).wait_recv()

    for mate in z_mates:
        pass_on(me, mate)
    pass_on(me, x_mate)
    pass_on(me, core_mate)
    arrived(x_mate, x_mate)
    pass_on(x_mate, core_mate)
    for d in range(1, num_z):
        block = device_at(z_behind(d), x, core)
        arrived(block, x_mate)
        pass_on(block, x_mate)
        pass_on(block, core_mate)
    for d in range(1, num_z):
        block = device_at(z_behind(d), 1 - x, core)
        arrived(block, x_mate)
        pass_on(block, core_mate)
    for at_z in range(num_z):
        for at_x in range(2):
            arrived(device_at(at_z, at_x, 1 - core), core_mate)
    for copy in posted + sent:
        copy.wait_send()

    all_in = tokens[...].reshape(rows, width)
    named = inbox[:, :, facts_at:].reshape(rows, 128).astype(jnp.float32)
    logits = dot(all_in, router_ref[...])
    lanes = lax.broadcasted_iota(jnp.int32, (rows, experts), 1).astype(jnp.float32)
    squashed = jnp.zeros((rows, experts), jnp.float32)
    chosen = jnp.zeros((rows, experts), jnp.float32)
    ids_at = 2 * value_heads
    for k in range(TOPK):
        chosen = jnp.where(named[:, ids_at + k : ids_at + k + 1] == lanes, 1.0, chosen)
    squashed = jnp.where(chosen > 0.5, jax.nn.sigmoid(logits), 0.0)
    gates = squashed / jnp.sum(squashed, axis=1, keepdims=True)
    gates_hi = gates.astype(jnp.bfloat16)
    gates_lo = (gates - gates_hi.astype(jnp.float32)).astype(jnp.bfloat16)
    mine = (
        lax.broadcasted_iota(jnp.int32, (local_experts, experts), 1)
        == lax.broadcasted_iota(jnp.int32, (local_experts, experts), 0) + me * local_experts
    )
    mine = jnp.where(mine, 1.0, 0.0).astype(jnp.bfloat16)
    hits = dot_nt(mine, chosen.astype(jnp.bfloat16))
    local_hi = dot_nt(mine, gates_hi)
    local_lo = dot_nt(mine, gates_lo)
    row_a = lax.broadcasted_iota(jnp.int32, (rows, rows), 0)
    row_b = lax.broadcasted_iota(jnp.int32, (rows, rows), 1)
    earlier = (row_a // owned == row_b // owned) & (row_a < row_b)
    rank = dot(hits.astype(jnp.bfloat16), jnp.where(earlier, 1.0, 0.0).astype(jnp.bfloat16))
    origin = lax.broadcasted_iota(jnp.int32, (local_experts, rows), 1) // owned
    place = jnp.where(hits > 0.5, (origin * CAP).astype(jnp.float32) + rank, -1.0)
    slots = CAP * wide_size
    slot_no = lax.broadcasted_iota(jnp.int32, (slots, rows), 0).astype(jnp.float32)
    takes, takes_hi, takes_lo = [], [], []
    for e in range(local_experts):
        taken = place[e : e + 1] == slot_no
        takes.append(jnp.where(taken, 1.0, 0.0))
        takes_hi.append(jnp.where(taken, local_hi[e : e + 1], 0.0))
        takes_lo.append(jnp.where(taken, local_lo[e : e + 1], 0.0))
    take = jnp.concatenate(takes, axis=0).astype(jnp.bfloat16)
    slab[...] = dot(take, all_in).astype(jnp.bfloat16).reshape(local_experts, slots, width)

    def back(pieces):
        turned = jnp.concatenate(pieces, axis=0).T.astype(jnp.bfloat16)
        return turned.reshape(num_z * 2, 2, owned, local_experts * slots)

    pick_hi[...] = back(takes_hi)
    pick_lo[...] = back(takes_lo)

    @pl.loop(0, local_experts)
    def _(e):
        slot = lax.rem(e, held)
        for copy in up_copies(e, slot):
            copy.wait()
        came = slab[e]
        gate_part = dot(came, gate_w[slot])
        up_part = dot(came, up_w[slot])
        mid[e] = (jax.nn.silu(gate_part) * up_part).astype(jnp.bfloat16)

        @pl.when(e + held < local_experts)
        def _():
            for copy in up_copies(e + held, slot):
                copy.start()

    for e in range(local_experts):
        down_copy(e).wait()

    def combine(c):
        cut = slice(c * wide_cut, (c + 1) * wide_cut)
        results = jnp.concatenate(
            [dot(mid[e], down_w[e, :, cut]).astype(jnp.bfloat16) for e in range(local_experts)],
            axis=0,
        )

        def sums(at_core):
            hi = pick_hi[:, at_core].reshape(half, local_experts * slots)
            lo = pick_lo[:, at_core].reshape(half, local_experts * slots)
            return dot(hi, results) + dot(lo, results)

        return sums

    result = reduce_scatter(1, combine) + hidden[...]
    for r in range(requests):
        mixed_ref[r] = result[r * num_steps : (r + 1) * num_steps].astype(mixed_ref.dtype)


def fused_layer(
    prefill_state,
    residual_in,
    queries,
    keys_in,
    values_in,
    gate_in,
    beta_rate,
    decay_rate,
    norm_gain,
    out_weight,
    post_gain,
    router_weight,
    expert_ids,
    expert_gate,
    expert_up,
    expert_down,
):
    wide_size = lax.axis_size("wide")
    owned_req, num_steps, width = residual_in.shape
    owned = owned_req * num_steps
    rows = wide_size * owned
    total_req, key_dim, columns = prefill_state.shape
    value_heads = beta_rate.shape[2]
    box = 2 * key_dim + 2 * columns + 128
    num_z = wide_size // 4
    experts = router_weight.shape[1]
    local_experts, _, hidden_units = expert_gate.shape
    held = min(local_experts, 6)
    slots = CAP * wide_size
    facts = jnp.concatenate(
        [beta_rate, decay_rate, expert_ids.astype(jnp.bfloat16)], axis=-1
    ).reshape(owned, 2 * value_heads + TOPK)
    facts = jnp.pad(facts, ((0, 0), (0, 128 - facts.shape[1])))
    chunks = 4
    cut = width // chunks
    half16 = (2, chunks, num_z, 2, owned, cut)
    bf16, f32 = jnp.bfloat16, jnp.float32
    vmem = pl.BlockSpec(memory_space=pltpu.VMEM)
    hbm = pl.BlockSpec(memory_space=pl.ANY)
    out = pl.pallas_call(
        functools.partial(
            layer_kernel, (wide_size, owned, width, experts, local_experts, held, chunks)
        ),
        out_shape=jax.ShapeDtypeStruct((owned_req, num_steps, width), bf16),
        in_specs=[hbm] + [vmem] * 10 + [hbm] * 3,
        out_specs=vmem,
        scratch_shapes=[
            pltpu.VMEM((wide_size, owned_req * key_dim, columns), bf16),
            pltpu.VMEM((wide_size, owned, box), bf16),
            pltpu.VMEM((wide_size, owned, box), bf16),
            pltpu.VMEM((wide_size, 2 * owned, columns), f32),
            pltpu.VMEM((num_z * 2, 2, owned, columns), bf16),
            pltpu.VMEM((held, width, hidden_units), bf16),
            pltpu.VMEM((held, width, hidden_units), bf16),
            pltpu.VMEM((local_experts, hidden_units, width), bf16),
            pltpu.VMEM(half16, bf16),
            pltpu.VMEM(half16, bf16),
            pltpu.VMEM((2, chunks, num_z, owned, cut), bf16),
            pltpu.VMEM((2, chunks, num_z, owned, cut), bf16),
            pltpu.VMEM((2, chunks, num_z - 1, owned, cut), bf16),
            pltpu.VMEM((2, chunks, num_z - 1, owned, cut), bf16),
            pltpu.VMEM((chunks, num_z, 2, owned, cut), f32),
            pltpu.VMEM((chunks, num_z, owned, cut), f32),
            pltpu.VMEM((owned, width), f32),
            pltpu.VMEM((wide_size, owned, width), bf16),
            pltpu.VMEM((local_experts, slots, width), bf16),
            pltpu.VMEM((local_experts, slots, hidden_units), bf16),
            pltpu.VMEM((num_z * 2, 2, owned, local_experts * slots), bf16),
            pltpu.VMEM((num_z * 2, 2, owned, local_experts * slots), bf16),
            pltpu.SemaphoreType.DMA,
            pltpu.SemaphoreType.DMA((wide_size - 1,)),
            pltpu.SemaphoreType.DMA((wide_size - 1,)),
            pltpu.SemaphoreType.DMA((2, held)),
            pltpu.SemaphoreType.DMA((local_experts,)),
            pltpu.SemaphoreType.DMA((2, chunks, 1 + num_z)),
            pltpu.SemaphoreType.DMA((2, chunks, 1 + num_z)),
            pltpu.SemaphoreType.DMA((wide_size,)),
            pltpu.SemaphoreType.DMA((wide_size,)),
        ],
        compiler_params=pltpu.CompilerParams(
            collective_id=0, has_side_effects=True, vmem_limit_bytes=62 * 1024 * 1024
        ),
    )(
        prefill_state.reshape(wide_size, owned_req * key_dim, columns),
        queries,
        keys_in,
        values_in,
        gate_in,
        facts,
        norm_gain.reshape(1, norm_gain.shape[0]),
        out_weight,
        residual_in,
        post_gain.reshape(1, width),
        router_weight,
        expert_gate,
        expert_up,
        expert_down,
    )
    return out


def per_device(
    prefill_state,
    residual_in,
    queries,
    keys_in,
    values_in,
    gate_in,
    beta_rate,
    decay_rate,
    norm_gain,
    out_weight,
    post_gain,
    router_weight,
    expert_ids,
    expert_gate,
    expert_up,
    expert_down,
):
    wide_size = lax.axis_size("wide")
    owned_req = queries.shape[0]
    num_steps = queries.shape[1]
    local_rows = owned_req * num_steps
    key_dim = prefill_state.shape[1]
    columns = prefill_state.shape[2]
    head_dim = norm_gain.shape[0]
    hv_dv = values_in.shape[2]
    value_heads = hv_dv // head_dim
    key_heads = queries.shape[2] // key_dim
    key_group = hv_dv // key_heads
    width = residual_in.shape[2]
    if key_heads == wide_size == 16 and local_rows == 16 and router_weight.shape[1] == 128:
        return fused_layer(
            prefill_state,
            residual_in,
            queries,
            keys_in,
            values_in,
            gate_in,
            beta_rate,
            decay_rate,
            norm_gain,
            out_weight,
            post_gain,
            router_weight,
            expert_ids,
            expert_gate,
            expert_up,
            expert_down,
        )
    heads = local_heads if key_heads == wide_size else moved_heads
    spread = heads(
        prefill_state, queries, keys_in, values_in, gate_in, beta_rate, decay_rate, norm_gain
    )
    attention = lax.psum_scatter(
        jnp.dot(spread, out_weight, preferred_element_type=jnp.float32),
        "wide",
        scatter_dimension=0,
        tiled=True,
    )
    hidden = residual_in.reshape(local_rows, width).astype(jnp.float32) + attention
    moe_in = (
        hidden * lax.rsqrt(jnp.mean(hidden * hidden, axis=-1, keepdims=True) + 1e-06) * post_gain
    ).astype(jnp.bfloat16)
    logits = jnp.dot(moe_in, router_weight, preferred_element_type=jnp.float32)
    num_experts = router_weight.shape[1]
    flat_ids = expert_ids.reshape(local_rows, TOPK)
    onehot = flat_ids[:, :, None] == jnp.arange(num_experts, dtype=jnp.int32)[None, None, :]
    chosen = jnp.sum(jnp.where(onehot, logits[:, None, :], 0.0), axis=-1)
    squashed = jax.nn.sigmoid(chosen)
    gates = squashed / jnp.sum(squashed, axis=1, keepdims=True)
    counts_flat = onehot.reshape(local_rows * TOPK, num_experts).astype(jnp.int32)
    running = jnp.cumsum(counts_flat, axis=0) - 1
    slot_of = jnp.sum(counts_flat * running, axis=1).reshape(local_rows, TOPK)
    position = flat_ids * CAP + slot_of
    dispatch = jnp.any(
        position[:, :, None] == jnp.arange(num_experts * CAP, dtype=jnp.int32)[None, None, :],
        axis=1,
    ).astype(jnp.bfloat16)
    buffer = jnp.einsum("rs,rd->sd", dispatch, moe_in, preferred_element_type=jnp.float32).astype(
        jnp.bfloat16
    )
    exp_dev = expert_gate.shape[0]
    buffer = buffer.reshape(wide_size, exp_dev, CAP, width)
    slab_in = lax.all_to_all(buffer, "wide", split_axis=0, concat_axis=0, tiled=True)
    gate_part = jnp.einsum(
        "sekd,edf->sekf", slab_in, expert_gate, preferred_element_type=jnp.float32
    )
    up_part = jnp.einsum("sekd,edf->sekf", slab_in, expert_up, preferred_element_type=jnp.float32)
    hidden_mid = (jax.nn.silu(gate_part) * up_part).astype(jnp.bfloat16)
    processed = jnp.einsum(
        "sekf,efd->sekd", hidden_mid, expert_down, preferred_element_type=jnp.float32
    ).astype(jnp.bfloat16)
    returned = lax.all_to_all(processed, "wide", split_axis=0, concat_axis=0, tiled=True).reshape(
        num_experts * CAP, width
    )
    picked = returned[position]
    combined = jnp.sum(gates[:, :, None] * picked.astype(jnp.float32), axis=1)
    return (hidden + combined).astype(jnp.bfloat16).reshape(owned_req, num_steps, width)


def solution(mesh):
    return jax.shard_map(
        per_device,
        mesh=mesh,
        in_specs=(
            P("groups", None, "wide"),
            P(("groups", "wide"), None, None),
            P(("groups", "wide"), None, None),
            P(("groups", "wide"), None, None),
            P(("groups", "wide"), None, None),
            P(("groups", "wide"), None, None),
            P(("groups", "wide"), None, None),
            P(("groups", "wide"), None, None),
            P(),
            P("wide", None),
            P(),
            P(),
            P(("groups", "wide"), None, None),
            P("wide", None, None),
            P("wide", None, None),
            P("wide", None, None),
        ),
        out_specs=P(("groups", "wide"), None, None),
        check_vma=False,
    )
```

```python
import functools

import jax
import jax.numpy as jnp
from jax import lax
from jax.experimental import pallas as pl
from jax.experimental.pallas import tpu as pltpu
from jax.sharding import PartitionSpec as P

TOPK = 10
CAP = 2


def unit_rows(vectors):
    vectors = vectors.astype(jnp.float32)
    return vectors * lax.rsqrt(jnp.sum(vectors * vectors, axis=-1, keepdims=True) + 1e-06)


def recurrence(carry_state, q_unit, k_unit, value_cols, beta_cols, decay_cols):
    results = []
    for step_idx in range(q_unit.shape[1]):
        carry_state = carry_state * decay_cols[:, step_idx][:, None]
        key_now = jnp.swapaxes(k_unit[:, step_idx], 1, 2)[..., None]
        predicted = jnp.einsum(
            "bdhc,bhd->bhc", carry_state, k_unit[:, step_idx], precision=lax.Precision.HIGHEST
        )
        change = beta_cols[:, step_idx] * (value_cols[:, step_idx] - predicted)
        carry_state = carry_state + key_now * change[:, None]
        results.append(
            jnp.einsum(
                "bdhc,bhd->bhc", carry_state, q_unit[:, step_idx], precision=lax.Precision.HIGHEST
            )
        )
    return jnp.stack(results, axis=1)


def local_heads(prefill_state, queries, keys_in, values_in, gate_in, beta_rate, decay_rate, norm_gain):
    owned_req, num_steps, _ = queries.shape
    total_req, key_dim, columns = prefill_state.shape
    head_dim = norm_gain.shape[0]
    wide_size = lax.axis_size("wide")
    group = columns // head_dim

    def by_head(array):
        return array.reshape(owned_req, num_steps, wide_size, -1)

    packed = jnp.concatenate(
        [by_head(a) for a in (queries, keys_in, values_in, gate_in, beta_rate, decay_rate)], axis=-1
    )
    got = lax.all_to_all(packed, "wide", split_axis=2, concat_axis=0, tiled=True)[:, :, 0]
    q_raw, k_raw, v_raw, g_raw, beta, decay = jnp.split(
        got,
        [key_dim, 2 * key_dim, 2 * key_dim + columns, 2 * key_dim + 2 * columns, 2 * key_dim + 2 * columns + group],
        axis=-1,
    )

    def inverse_norm(vectors):
        vectors = vectors.astype(jnp.float32)
        return lax.rsqrt(jnp.sum(vectors * vectors, axis=-1) + 1e-06)

    q_inv, k_inv = inverse_norm(q_raw), inverse_norm(k_raw)
    both = jnp.concatenate([k_raw, q_raw], axis=1)
    from_state = jnp.einsum("rsd,rdc->rsc", both, prefill_state, preferred_element_type=jnp.float32)
    gram = jnp.einsum("rsd,rtd->rst", both, k_raw, preferred_element_type=jnp.float32)
    gram = gram * jnp.concatenate([k_inv, q_inv], axis=1)[:, :, None] * k_inv[:, None, :]
    from_state = from_state * jnp.concatenate([k_inv, q_inv], axis=1)[:, :, None]

    def widen(rates):
        return jnp.repeat(rates.astype(jnp.float32), head_dim, axis=-1)

    beta, decay = widen(beta), widen(decay)
    value_cols = v_raw.astype(jnp.float32)
    through = jnp.ones_like(decay[:, 0])
    changes, results = [], []
    for t in range(num_steps):
        through = through * decay[:, t]
        changes = [c * decay[:, t] for c in changes]
        predicted = through * from_state[:, t]
        attended = through * from_state[:, num_steps + t]
        for s, c in enumerate(changes):
            predicted = predicted + gram[:, t, s][:, None] * c
            attended = attended + gram[:, num_steps + t, s][:, None] * c
        now = beta[:, t] * (value_cols[:, t] - predicted)
        attended = attended + gram[:, num_steps + t, t][:, None] * now
        changes.append(now)
        results.append(attended)
    heads_view = jnp.stack(results, axis=1).reshape(total_req * num_steps, group, head_dim)
    scale = lax.rsqrt(jnp.mean(heads_view * heads_view, axis=-1, keepdims=True) + 1e-06)
    gate_act = jax.nn.silu(g_raw.astype(jnp.float32)).reshape(heads_view.shape)
    normed = (heads_view * scale * norm_gain * gate_act).astype(jnp.bfloat16)
    return normed.reshape(total_req * num_steps, columns)


def moved_heads(prefill_state, queries, keys_in, values_in, gate_in, beta_rate, decay_rate, norm_gain):
    wide_size = lax.axis_size("wide")
    owned_req = queries.shape[0]
    num_steps = queries.shape[1]
    local_rows = owned_req * num_steps
    key_dim = prefill_state.shape[1]
    columns = prefill_state.shape[2]
    head_dim = norm_gain.shape[0]
    hv_dv = values_in.shape[2]
    value_heads = hv_dv // head_dim
    key_heads = queries.shape[2] // key_dim
    key_group = hv_dv // key_heads
    arrived = lax.all_to_all(prefill_state, "wide", split_axis=0, concat_axis=2, tiled=True)
    carry_state = arrived.astype(jnp.float32).reshape(owned_req, key_dim, key_heads, key_group)
    q_unit = unit_rows(queries.reshape(owned_req, num_steps, key_heads, key_dim))
    k_unit = unit_rows(keys_in.reshape(owned_req, num_steps, key_heads, key_dim))
    value_cols = values_in.astype(jnp.float32).reshape(owned_req, num_steps, key_heads, key_group)
    beta_cols = jnp.repeat(beta_rate.astype(jnp.float32), head_dim, axis=-1).reshape(
        owned_req, num_steps, key_heads, key_group
    )
    decay_cols = jnp.repeat(decay_rate.astype(jnp.float32), head_dim, axis=-1).reshape(
        owned_req, num_steps, key_heads, key_group
    )
    attended = recurrence(carry_state, q_unit, k_unit, value_cols, beta_cols, decay_cols).reshape(
        local_rows, hv_dv
    )
    heads_view = attended.reshape(local_rows, value_heads, head_dim)
    scale = lax.rsqrt(jnp.mean(heads_view * heads_view, axis=-1, keepdims=True) + 1e-06)
    gate_act = jax.nn.silu(gate_in.reshape(local_rows, value_heads, head_dim).astype(jnp.float32))
    normed = (
        (heads_view * scale * norm_gain * gate_act).astype(jnp.bfloat16).reshape(local_rows, hv_dv)
    )
    return lax.all_to_all(
        normed.reshape(local_rows, wide_size, columns),
        "wide",
        split_axis=1,
        concat_axis=0,
        tiled=True,
    ).reshape(wide_size * local_rows, columns)


def dot(left, right):
    return jnp.dot(left, right, preferred_element_type=jnp.float32)


def dot_nt(left, right):
    return lax.dot_general(
        left, right, (((1,), (1,)), ((), ())), preferred_element_type=jnp.float32
    )


def layer_kernel(
    sizes,
    state_hbm,
    q_hbm,
    k_hbm,
    v_hbm,
    g_hbm,
    facts_ref,
    gain_ref,
    out_w_hbm,
    resid_hbm,
    post_ref,
    router_hbm,
    gate_hbm,
    up_hbm,
    down_hbm,
    mixed_ref,
    q_ref,
    k_ref,
    v_ref,
    g_ref,
    out_w_ref,
    resid_ref,
    router_ref,
    state,
    outbox,
    inbox,
    from_state,
    heads,
    gate_w,
    up_w,
    down_w,
    core_send,
    core_recv,
    x_send,
    x_recv,
    z_send,
    z_recv,
    part,
    lane_part,
    hidden,
    tokens,
    slab,
    mid,
    pick_hi,
    pick_lo,
    early_sem,
    state_sem,
    box_send_sem,
    box_recv_sem,
    w_sem,
    down_sem,
    rs_send_sem,
    rs_recv_sem,
    ag_send_sem,
    ag_recv_sem,
):
    wide_size, owned, width, experts, local_experts, held, chunks = sizes
    num_z = wide_size // 4
    rows = wide_size * owned
    half = rows // 2
    me = lax.axis_index("wide")
    core = lax.rem(me, 2)
    x = lax.rem(me // 2, 2)
    z = me // 4

    def device_at(at_z, at_x, at_core):
        return at_z * 4 + at_x * 2 + at_core

    def z_ahead(d):
        return lax.rem(z + d, num_z)

    def z_behind(d):
        return lax.rem(z + num_z - d, num_z)

    core_mate = device_at(z, x, 1 - core)
    x_mate = device_at(z, 1 - x, core)
    z_mates = [device_at(z_ahead(d), x, core) for d in range(1, num_z)]

    def up_copies(e, slot):
        return [
            pltpu.make_async_copy(hbm.at[e], vmem.at[slot], w_sem.at[i, slot])
            for i, (hbm, vmem) in enumerate(((gate_hbm, gate_w), (up_hbm, up_w)))
        ]

    def down_copy(e):
        return pltpu.make_async_copy(down_hbm.at[e], down_w.at[e], down_sem.at[e])

    early = [
        pltpu.make_async_copy(source, held_here, early_sem.at[i])
        for i, (source, held_here) in enumerate(
            (
                (q_hbm, q_ref),
                (k_hbm, k_ref),
                (v_hbm, v_ref),
                (g_hbm, g_ref),
                (out_w_hbm, out_w_ref),
                (resid_hbm, resid_ref),
                (router_hbm, router_ref),
            )
        )
    ]
    for copy in early:
        copy.start()
    state_copy = pltpu.make_async_copy(state_hbm, state, state_sem)
    state_copy.start()
    barrier = pltpu.get_barrier_semaphore()
    moves = [(dz, dx, dc) for dz in range(num_z) for dx in range(2) for dc in range(2)][1:]

    def offset(at_z, dx, dc):
        return device_at(at_z, 1 - x if dx else x, 1 - core if dc else core)

    for dz, dx, dc in moves:
        mate = offset(z_ahead(dz), dx, dc)
        pl.semaphore_signal(
            barrier, inc=1, device_id={"wide": mate}, device_id_type=pl.DeviceIdType.MESH
        )
    requests, num_steps, _ = q_ref.shape

    def flat(ref):
        return jnp.concatenate([ref[r].astype(jnp.float32) for r in range(requests)], axis=0)

    for copy in early[:4]:
        copy.wait()
    fields = []
    for ref in (q_ref, k_ref, v_ref, g_ref):
        values = flat(ref).astype(jnp.bfloat16)
        size = values.shape[1] // wide_size
        at = sum(fields)
        for to in range(wide_size):
            outbox[to, :, at : at + size] = values[:, to * size : (to + 1) * size]
        fields.append(size)
    key_dim, columns = fields[0], fields[2]
    values_at, gate_at, facts_at = 2 * key_dim, 2 * key_dim + columns, sum(fields)
    for to in range(wide_size):
        outbox[to, :, facts_at:] = facts_ref[...]
    pl.semaphore_wait(barrier, wide_size - 1)

    def remote(src, dst, send_sem, recv_sem, mate):
        return pltpu.make_async_remote_copy(
            src_ref=src,
            dst_ref=dst,
            send_sem=send_sem,
            recv_sem=recv_sem,
            device_id={"wide": mate},
            device_id_type=pl.DeviceIdType.MESH,
        )

    posted = []
    for i in reversed(range(len(moves))):
        dz, dx, dc = moves[i]
        mate = offset(z_ahead(dz), dx, dc)
        copy = remote(
            outbox.at[mate], inbox.at[me], box_send_sem.at[i], box_recv_sem.at[i], mate
        )
        copy.start()
        posted.insert(0, copy)
    inbox[me] = outbox[me]
    state_copy.wait()
    of_request = lax.broadcasted_iota(jnp.int32, (2 * owned, requests * key_dim), 0) % owned
    of_lane = lax.broadcasted_iota(jnp.int32, (2 * owned, requests * key_dim), 1)
    own_state = jnp.where(of_request // num_steps == of_lane // key_dim, 1.0, 0.0)
    own_state = own_state.astype(jnp.bfloat16)

    def meet_state(block):
        came = inbox[block]
        pair = jnp.concatenate([came[:, key_dim : 2 * key_dim], came[:, :key_dim]], axis=0)
        spaced = jnp.concatenate([pair] * requests, axis=1) * own_state
        from_state[block] = dot(spaced, state[block])

    meet_state(me)
    for i, (dz, dx, dc) in enumerate(moves):
        posted[i].wait_recv()
        meet_state(offset(z_behind(dz), dx, dc))

    for e in range(held):
        for copy in up_copies(e, e):
            copy.start()
    for e in range(local_experts):
        down_copy(e).start()

    at_once = 4
    many = at_once * owned
    head_dim = gain_ref.shape[1]
    group = columns // head_dim
    value_heads = group * wide_size
    step = lax.broadcasted_iota(jnp.int32, (many, head_dim), 0) % num_steps
    step_col = step[:, :1]
    lane = lax.broadcasted_iota(jnp.int32, (many, 128), 1)

    def unit(vectors):
        return lax.rsqrt(jnp.sum(vectors * vectors, axis=1, keepdims=True) + 1e-06)

    def before(array, d):
        return pltpu.roll(array, d, 0) if d else array

    for first in range(0, wide_size, at_once):
        came = inbox[first : first + at_once].reshape(many, inbox.shape[-1])
        q_raw = came[:, :key_dim].astype(jnp.float32)
        k_raw = came[:, key_dim : 2 * key_dim].astype(jnp.float32)
        q_inv, k_inv = unit(q_raw), unit(k_raw)
        q_unit, k_unit = q_raw * q_inv, k_raw * k_inv
        met = from_state[first : first + at_once]
        k_met = met[:, :owned].reshape(many, columns) * k_inv
        q_met = met[:, owned:].reshape(many, columns) * q_inv
        kk, qk = [], []
        for d in range(num_steps):
            earlier = before(k_unit, d)
            valid = step_col >= d
            kk.append(
                jnp.where(valid, jnp.sum(k_unit * earlier, axis=1, keepdims=True), 0.0)
            )
            qk.append(
                jnp.where(valid, jnp.sum(q_unit * earlier, axis=1, keepdims=True), 0.0)
            )
        facts = came[:, facts_at:].astype(jnp.float32)
        for j in range(group):
            cut = slice(j * head_dim, (j + 1) * head_dim)
            head = me * group + j
            beta = jnp.sum(jnp.where(lane == head, facts, 0.0), axis=1, keepdims=True)
            decay = jnp.sum(
                jnp.where(lane == head + value_heads, facts, 0.0), axis=1, keepdims=True
            )
            decay = jnp.broadcast_to(decay, (many, head_dim))
            kept = [None, decay]
            for d in range(1, num_steps):
                kept.append(kept[d] * before(decay, d))
            through = decay
            for t in range(1, num_steps):
                through = jnp.where(step == t, kept[t + 1], through)
            value_cols = came[:, values_at:gate_at][:, cut].astype(jnp.float32)
            base = value_cols - through * k_met[:, cut]
            change = beta * base
            for _ in range(1, num_steps):
                rest = base
                for d in range(1, num_steps):
                    rest = rest - kept[d] * kk[d] * before(change, d)
                change = beta * rest
            attended = through * q_met[:, cut] + qk[0] * change
            for d in range(1, num_steps):
                attended = attended + kept[d] * qk[d] * before(change, d)
            scale = lax.rsqrt(jnp.mean(attended * attended, axis=1, keepdims=True) + 1e-06)
            gate_act = jax.nn.silu(came[:, gate_at:facts_at][:, cut].astype(jnp.float32))
            normed = (attended * scale * gain_ref[...] * gate_act).astype(jnp.bfloat16)
            heads[first // 2 : (first + at_once) // 2, :, :, cut] = normed.reshape(
                at_once // 2, 2, owned, head_dim
            )

    for copy in early[4:]:
        copy.wait()
    wide_cut = width // chunks

    def reduce_scatter(turn, produce):
        started = {}

        def exchange(c, i, src, dst, mate):
            copy = remote(src, dst, rs_send_sem.at[turn, c, i], rs_recv_sem.at[turn, c, i], mate)
            copy.start()
            started[c, i] = copy

        def over_cores(c):
            sums = produce(c)
            core_send[turn, c] = (
                sums(1 - core).astype(jnp.bfloat16).reshape(num_z, 2, owned, wide_cut)
            )
            exchange(c, 0, core_send.at[turn, c], core_recv.at[turn, c], core_mate)
            part[c] = sums(core).reshape(num_z, 2, owned, wide_cut)

        def over_x(c):
            started[c, 0].wait_recv()
            x_send[turn, c] = (
                part[c, :, 1 - x] + core_recv[turn, c, :, 1 - x].astype(jnp.float32)
            ).astype(jnp.bfloat16)
            exchange(c, 1, x_send.at[turn, c], x_recv.at[turn, c], x_mate)
            lane_part[c] = part[c, :, x] + core_recv[turn, c, :, x].astype(jnp.float32)

        def over_z(c):
            started[c, 1].wait_recv()
            for d in range(1, num_z):
                at_z = z_ahead(d)
                z_send[turn, c, d - 1] = (
                    lane_part[c, at_z] + x_recv[turn, c, at_z].astype(jnp.float32)
                ).astype(jnp.bfloat16)
                exchange(
                    c, 1 + d, z_send.at[turn, c, d - 1], z_recv.at[turn, c, d - 1], z_mates[d - 1]
                )

        def total(c):
            value = lane_part[c, z] + x_recv[turn, c, z].astype(jnp.float32)
            for d in range(1, num_z):
                started[c, 1 + d].wait_recv()
                value = value + z_recv[turn, c, d - 1].astype(jnp.float32)
            return value

        totals = []
        for tick in range(chunks + 3):
            for late, stage in enumerate((over_cores, over_x, over_z)):
                if 0 <= tick - late < chunks:
                    stage(tick - late)
            if tick >= 3:
                totals.append(total(tick - 3))
        for copy in started.values():
            copy.wait_send()
        return jnp.concatenate(totals, axis=1)

    def project(c):
        weights = out_w_ref[:, c * wide_cut : (c + 1) * wide_cut]
        return lambda at_core: dot(heads[:, at_core].reshape(half, columns), weights)

    now = flat(resid_ref) + reduce_scatter(0, project)
    hidden[...] = now
    moe_in = now * lax.rsqrt(jnp.mean(now * now, axis=-1, keepdims=True) + 1e-06) * post_ref[...]
    tokens[me] = moe_in.astype(jnp.bfloat16)

    sent = []

    def pass_on(block, mate):
        copy = remote(
            tokens.at[block],
            tokens.at[block],
            ag_send_sem.at[len(sent)],
            ag_recv_sem.at[block],
            mate,
        )
        copy.start()
        sent.append(copy)

    def arrived(block, mate):
        remote(
            tokens.at[block], tokens.at[block], ag_send_sem.at[0], ag_recv_sem.at[block], mate
        ).wait_recv()

    for mate in z_mates:
        pass_on(me, mate)
    pass_on(me, x_mate)
    pass_on(me, core_mate)
    arrived(x_mate, x_mate)
    pass_on(x_mate, core_mate)
    for d in range(1, num_z):
        block = device_at(z_behind(d), x, core)
        arrived(block, x_mate)
        pass_on(block, x_mate)
        pass_on(block, core_mate)
    for d in range(1, num_z):
        block = device_at(z_behind(d), 1 - x, core)
        arrived(block, x_mate)
        pass_on(block, core_mate)
    for at_z in range(num_z):
        for at_x in range(2):
            arrived(device_at(at_z, at_x, 1 - core), core_mate)
    for copy in posted + sent:
        copy.wait_send()

    all_in = tokens[...].reshape(rows, width)
    named = inbox[:, :, facts_at:].reshape(rows, 128).astype(jnp.float32)
    logits = dot(all_in, router_ref[...])
    lanes = lax.broadcasted_iota(jnp.int32, (rows, experts), 1).astype(jnp.float32)
    squashed = jnp.zeros((rows, experts), jnp.float32)
    chosen = jnp.zeros((rows, experts), jnp.float32)
    ids_at = 2 * value_heads
    for k in range(TOPK):
        chosen = jnp.where(named[:, ids_at + k : ids_at + k + 1] == lanes, 1.0, chosen)
    squashed = jnp.where(chosen > 0.5, jax.nn.sigmoid(logits), 0.0)
    gates = squashed / jnp.sum(squashed, axis=1, keepdims=True)
    gates_hi = gates.astype(jnp.bfloat16)
    gates_lo = (gates - gates_hi.astype(jnp.float32)).astype(jnp.bfloat16)
    mine = (
        lax.broadcasted_iota(jnp.int32, (local_experts, experts), 1)
        == lax.broadcasted_iota(jnp.int32, (local_experts, experts), 0) + me * local_experts
    )
    mine = jnp.where(mine, 1.0, 0.0).astype(jnp.bfloat16)
    hits = dot_nt(mine, chosen.astype(jnp.bfloat16))
    local_hi = dot_nt(mine, gates_hi)
    local_lo = dot_nt(mine, gates_lo)
    row_a = lax.broadcasted_iota(jnp.int32, (rows, rows), 0)
    row_b = lax.broadcasted_iota(jnp.int32, (rows, rows), 1)
    earlier = (row_a // owned == row_b // owned) & (row_a < row_b)
    rank = dot(hits.astype(jnp.bfloat16), jnp.where(earlier, 1.0, 0.0).astype(jnp.bfloat16))
    origin = lax.broadcasted_iota(jnp.int32, (local_experts, rows), 1) // owned
    place = jnp.where(hits > 0.5, (origin * CAP).astype(jnp.float32) + rank, -1.0)
    slots = CAP * wide_size
    slot_no = lax.broadcasted_iota(jnp.int32, (slots, rows), 0).astype(jnp.float32)
    takes, takes_hi, takes_lo = [], [], []
    for e in range(local_experts):
        taken = place[e : e + 1] == slot_no
        takes.append(jnp.where(taken, 1.0, 0.0))
        takes_hi.append(jnp.where(taken, local_hi[e : e + 1], 0.0))
        takes_lo.append(jnp.where(taken, local_lo[e : e + 1], 0.0))
    take = jnp.concatenate(takes, axis=0).astype(jnp.bfloat16)
    slab[...] = dot(take, all_in).astype(jnp.bfloat16).reshape(local_experts, slots, width)

    def back(pieces):
        turned = jnp.concatenate(pieces, axis=0).T.astype(jnp.bfloat16)
        return turned.reshape(num_z * 2, 2, owned, local_experts * slots)

    pick_hi[...] = back(takes_hi)
    pick_lo[...] = back(takes_lo)

    @pl.loop(0, local_experts)
    def _(e):
        slot = lax.rem(e, held)
        for copy in up_copies(e, slot):
            copy.wait()
        came = slab[e]
        gate_part = dot(came, gate_w[slot])
        up_part = dot(came, up_w[slot])
        mid[e] = (jax.nn.silu(gate_part) * up_part).astype(jnp.bfloat16)

        @pl.when(e + held < local_experts)
        def _():
            for copy in up_copies(e + held, slot):
                copy.start()

    for e in range(local_experts):
        down_copy(e).wait()

    def combine(c):
        cut = slice(c * wide_cut, (c + 1) * wide_cut)
        results = jnp.concatenate(
            [dot(mid[e], down_w[e, :, cut]).astype(jnp.bfloat16) for e in range(local_experts)],
            axis=0,
        )

        def sums(at_core):
            hi = pick_hi[:, at_core].reshape(half, local_experts * slots)
            lo = pick_lo[:, at_core].reshape(half, local_experts * slots)
            return dot(hi, results) + dot(lo, results)

        return sums

    result = reduce_scatter(1, combine) + hidden[...]
    for r in range(requests):
        mixed_ref[r] = result[r * num_steps : (r + 1) * num_steps].astype(mixed_ref.dtype)


def fused_layer(
    prefill_state,
    residual_in,
    queries,
    keys_in,
    values_in,
    gate_in,
    beta_rate,
    decay_rate,
    norm_gain,
    out_weight,
    post_gain,
    router_weight,
    expert_ids,
    expert_gate,
    expert_up,
    expert_down,
):
    wide_size = lax.axis_size("wide")
    owned_req, num_steps, width = residual_in.shape
    owned = owned_req * num_steps
    rows = wide_size * owned
    total_req, key_dim, columns = prefill_state.shape
    value_heads = beta_rate.shape[2]
    box = 2 * key_dim + 2 * columns + 128
    num_z = wide_size // 4
    experts = router_weight.shape[1]
    local_experts, _, hidden_units = expert_gate.shape
    held = min(local_experts, 6)
    slots = CAP * wide_size
    facts = jnp.concatenate(
        [beta_rate, decay_rate, expert_ids.astype(jnp.bfloat16)], axis=-1
    ).reshape(owned, 2 * value_heads + TOPK)
    facts = jnp.pad(facts, ((0, 0), (0, 128 - facts.shape[1])))
    chunks = 4
    cut = width // chunks
    half16 = (2, chunks, num_z, 2, owned, cut)
    bf16, f32 = jnp.bfloat16, jnp.float32
    vmem = pl.BlockSpec(memory_space=pltpu.VMEM)
    hbm = pl.BlockSpec(memory_space=pl.ANY)
    out = pl.pallas_call(
        functools.partial(
            layer_kernel, (wide_size, owned, width, experts, local_experts, held, chunks)
        ),
        out_shape=jax.ShapeDtypeStruct((owned_req, num_steps, width), bf16),
        in_specs=[hbm] * 5 + [vmem] * 2 + [hbm] * 2 + [vmem] + [hbm] * 4,
        out_specs=vmem,
        scratch_shapes=[
            pltpu.VMEM(queries.shape, bf16),
            pltpu.VMEM(keys_in.shape, bf16),
            pltpu.VMEM(values_in.shape, bf16),
            pltpu.VMEM(gate_in.shape, bf16),
            pltpu.VMEM(out_weight.shape, bf16),
            pltpu.VMEM(residual_in.shape, bf16),
            pltpu.VMEM(router_weight.shape, bf16),
            pltpu.VMEM((wide_size, owned_req * key_dim, columns), bf16),
            pltpu.VMEM((wide_size, owned, box), bf16),
            pltpu.VMEM((wide_size, owned, box), bf16),
            pltpu.VMEM((wide_size, 2 * owned, columns), f32),
            pltpu.VMEM((num_z * 2, 2, owned, columns), bf16),
            pltpu.VMEM((held, width, hidden_units), bf16),
            pltpu.VMEM((held, width, hidden_units), bf16),
            pltpu.VMEM((local_experts, hidden_units, width), bf16),
            pltpu.VMEM(half16, bf16),
            pltpu.VMEM(half16, bf16),
            pltpu.VMEM((2, chunks, num_z, owned, cut), bf16),
            pltpu.VMEM((2, chunks, num_z, owned, cut), bf16),
            pltpu.VMEM((2, chunks, num_z - 1, owned, cut), bf16),
            pltpu.VMEM((2, chunks, num_z - 1, owned, cut), bf16),
            pltpu.VMEM((chunks, num_z, 2, owned, cut), f32),
            pltpu.VMEM((chunks, num_z, owned, cut), f32),
            pltpu.VMEM((owned, width), f32),
            pltpu.VMEM((wide_size, owned, width), bf16),
            pltpu.VMEM((local_experts, slots, width), bf16),
            pltpu.VMEM((local_experts, slots, hidden_units), bf16),
            pltpu.VMEM((num_z * 2, 2, owned, local_experts * slots), bf16),
            pltpu.VMEM((num_z * 2, 2, owned, local_experts * slots), bf16),
            pltpu.SemaphoreType.DMA((7,)),
            pltpu.SemaphoreType.DMA,
            pltpu.SemaphoreType.DMA((wide_size - 1,)),
            pltpu.SemaphoreType.DMA((wide_size - 1,)),
            pltpu.SemaphoreType.DMA((2, held)),
            pltpu.SemaphoreType.DMA((local_experts,)),
            pltpu.SemaphoreType.DMA((2, chunks, 1 + num_z)),
            pltpu.SemaphoreType.DMA((2, chunks, 1 + num_z)),
            pltpu.SemaphoreType.DMA((wide_size,)),
            pltpu.SemaphoreType.DMA((wide_size,)),
        ],
        compiler_params=pltpu.CompilerParams(
            collective_id=0, has_side_effects=True, vmem_limit_bytes=62 * 1024 * 1024
        ),
    )(
        prefill_state.reshape(wide_size, owned_req * key_dim, columns),
        queries,
        keys_in,
        values_in,
        gate_in,
        facts,
        norm_gain.reshape(1, norm_gain.shape[0]),
        out_weight,
        residual_in,
        post_gain.reshape(1, width),
        router_weight,
        expert_gate,
        expert_up,
        expert_down,
    )
    return out


def per_device(
    prefill_state,
    residual_in,
    queries,
    keys_in,
    values_in,
    gate_in,
    beta_rate,
    decay_rate,
    norm_gain,
    out_weight,
    post_gain,
    router_weight,
    expert_ids,
    expert_gate,
    expert_up,
    expert_down,
):
    wide_size = lax.axis_size("wide")
    owned_req = queries.shape[0]
    num_steps = queries.shape[1]
    local_rows = owned_req * num_steps
    key_dim = prefill_state.shape[1]
    columns = prefill_state.shape[2]
    head_dim = norm_gain.shape[0]
    hv_dv = values_in.shape[2]
    value_heads = hv_dv // head_dim
    key_heads = queries.shape[2] // key_dim
    key_group = hv_dv // key_heads
    width = residual_in.shape[2]
    if key_heads == wide_size == 16 and local_rows == 16 and router_weight.shape[1] == 128:
        return fused_layer(
            prefill_state,
            residual_in,
            queries,
            keys_in,
            values_in,
            gate_in,
            beta_rate,
            decay_rate,
            norm_gain,
            out_weight,
            post_gain,
            router_weight,
            expert_ids,
            expert_gate,
            expert_up,
            expert_down,
        )
    heads = local_heads if key_heads == wide_size else moved_heads
    spread = heads(
        prefill_state, queries, keys_in, values_in, gate_in, beta_rate, decay_rate, norm_gain
    )
    attention = lax.psum_scatter(
        jnp.dot(spread, out_weight, preferred_element_type=jnp.float32),
        "wide",
        scatter_dimension=0,
        tiled=True,
    )
    hidden = residual_in.reshape(local_rows, width).astype(jnp.float32) + attention
    moe_in = (
        hidden * lax.rsqrt(jnp.mean(hidden * hidden, axis=-1, keepdims=True) + 1e-06) * post_gain
    ).astype(jnp.bfloat16)
    logits = jnp.dot(moe_in, router_weight, preferred_element_type=jnp.float32)
    num_experts = router_weight.shape[1]
    flat_ids = expert_ids.reshape(local_rows, TOPK)
    onehot = flat_ids[:, :, None] == jnp.arange(num_experts, dtype=jnp.int32)[None, None, :]
    chosen = jnp.sum(jnp.where(onehot, logits[:, None, :], 0.0), axis=-1)
    squashed = jax.nn.sigmoid(chosen)
    gates = squashed / jnp.sum(squashed, axis=1, keepdims=True)
    counts_flat = onehot.reshape(local_rows * TOPK, num_experts).astype(jnp.int32)
    running = jnp.cumsum(counts_flat, axis=0) - 1
    slot_of = jnp.sum(counts_flat * running, axis=1).reshape(local_rows, TOPK)
    position = flat_ids * CAP + slot_of
    dispatch = jnp.any(
        position[:, :, None] == jnp.arange(num_experts * CAP, dtype=jnp.int32)[None, None, :],
        axis=1,
    ).astype(jnp.bfloat16)
    buffer = jnp.einsum("rs,rd->sd", dispatch, moe_in, preferred_element_type=jnp.float32).astype(
        jnp.bfloat16
    )
    exp_dev = expert_gate.shape[0]
    buffer = buffer.reshape(wide_size, exp_dev, CAP, width)
    slab_in = lax.all_to_all(buffer, "wide", split_axis=0, concat_axis=0, tiled=True)
    gate_part = jnp.einsum(
        "sekd,edf->sekf", slab_in, expert_gate, preferred_element_type=jnp.float32
    )
    up_part = jnp.einsum("sekd,edf->sekf", slab_in, expert_up, preferred_element_type=jnp.float32)
    hidden_mid = (jax.nn.silu(gate_part) * up_part).astype(jnp.bfloat16)
    processed = jnp.einsum(
        "sekf,efd->sekd", hidden_mid, expert_down, preferred_element_type=jnp.float32
    ).astype(jnp.bfloat16)
    returned = lax.all_to_all(processed, "wide", split_axis=0, concat_axis=0, tiled=True).reshape(
        num_experts * CAP, width
    )
    picked = returned[position]
    combined = jnp.sum(gates[:, :, None] * picked.astype(jnp.float32), axis=1)
    return (hidden + combined).astype(jnp.bfloat16).reshape(owned_req, num_steps, width)


def solution(mesh):
    return jax.shard_map(
        per_device,
        mesh=mesh,
        in_specs=(
            P("groups", None, "wide"),
            P(("groups", "wide"), None, None),
            P(("groups", "wide"), None, None),
            P(("groups", "wide"), None, None),
            P(("groups", "wide"), None, None),
            P(("groups", "wide"), None, None),
            P(("groups", "wide"), None, None),
            P(("groups", "wide"), None, None),
            P(),
            P("wide", None),
            P(),
            P(),
            P(("groups", "wide"), None, None),
            P("wide", None, None),
            P("wide", None, None),
            P("wide", None, None),
        ),
        out_specs=P(("groups", "wide"), None, None),
        check_vma=False,
    )
```
